768 devices in a mesh: px: 16 (over y_hi, x, core), py: 48 (over y_lo, z).
Axes of the slice: x: 4, y: 8 (y_hi: 2, y_lo: 4; y = y_hi * 4 + y_lo), z: 12, core: 2. Of those that a mesh axis runs over, the one named last changes fastest.
Arguments:
- features: bfloat16 [64, 384, 128], P('px', 'py'), may hold values from -6 to 6
- pair_mask: int32 [64, 384, 3], P('px', 'py'), may hold values 0 or 1
- w_update: bfloat16 [128, 128], replicated, may hold values from -0.21875 to 0.21875
- w_atom: bfloat16 [128, 128], replicated, may hold values from -0.5 to 0.5
- w_pair: bfloat16 [128, 128], replicated, may hold values from -0.5 to 0.5
- slot_bias: float32 [4, 128], replicated, may hold values from -4 to 4
- w_block: bfloat16 [128, 169], replicated, may hold values from -0.5 to 0.5
- trial: float32 [64, 384, 13, 256], P('px', 'py'), may hold values from -6 to 6
Outputs:
- filtered: float32 [64, 384, 13, 256], P('px', 'py')
The draws below stay inside these ranges and needn't reach their ends.
All inputs are finite; a program needn't handle non-finite values. No bound on the sum of `pair_mask` on one device may be relied on, other than what follows from the above.
Results may differ from the reference program's by a relative error of at most 0.0046.
Values may be sent and summed in bfloat16 or wider, within the bound.
A program may use at most 64 MiB of HBM per device.

```python
import jax
import jax.numpy as jnp
from jax import lax

CHANNELS = 128
HIDDEN_SIZE = 128
ORBITALS = 13
VECTORS = 256
STEPS = 3
ATOM_ROWS = 64
ATOM_COLS = 384


def with_ends(values, stream_key, least, high):
    longest = values.shape.index(max(values.shape))
    spots = []
    for shift in (0, 1):
        where = [jax.random.randint(jax.random.fold_in(stream_key, axis), (), 0, length) for axis, length in enumerate(values.shape)]
        where[longest] = (where[longest] + shift) % values.shape[longest]
        spots.append(tuple(where))
    return values.at[spots[0]].set(least).at[spots[1]].set(high)


def levels(rng, dims, pieces, smallest, top_value):
    level, own = 1.0, jax.random.fold_in(rng, 6)
    for axis_at, parts in pieces:
        draws = jnp.exp(jax.random.uniform(jax.random.fold_in(own, axis_at), (parts,), jnp.float32, smallest / len(pieces), top_value / len(pieces)))
        level = level * jnp.repeat(draws, dims[axis_at] // parts).reshape([-1 if axis == axis_at else 1 for axis in range(len(dims))])
    return level


def gaussian(own_key, extent, deviation, bound, pieces=(), held_as=jnp.bfloat16):
    level = levels(own_key, extent, pieces, -0.22, 0.18) if pieces else 1.0
    entries = jax.random.normal(own_key, extent, jnp.float32) * deviation * level
    return jnp.minimum(jnp.maximum(entries, -bound), bound).astype(held_as)


def setup_inputs(seed: int = 0) -> dict:
    key_list = jax.random.split(jax.random.key(seed), 9)
    return {
        "features": gaussian(key_list[0], (ATOM_ROWS, ATOM_COLS, CHANNELS), 1.0, 6.0, ((0, 16), (1, 48))),
        "pair_mask": with_ends((jax.random.randint(key_list[1], (ATOM_ROWS, ATOM_COLS, 3), 0, 4) < 3).astype(jnp.int32), jax.random.fold_in(key_list[1], 1), 0, 1),
        "w_update": gaussian(key_list[2], (CHANNELS, CHANNELS), (6 * CHANNELS) ** -0.5, 0.21875),
        "w_atom": gaussian(key_list[3], (CHANNELS, HIDDEN_SIZE), CHANNELS ** -0.5, 0.5),
        "w_pair": gaussian(key_list[4], (CHANNELS, HIDDEN_SIZE), CHANNELS ** -0.5, 0.5),
        "slot_bias": gaussian(key_list[5], (4, HIDDEN_SIZE), 1.0, 4.0, (), jnp.float32),
        "w_block": gaussian(key_list[6], (HIDDEN_SIZE, ORBITALS * ORBITALS), HIDDEN_SIZE ** -0.5, 0.5),
        "trial": gaussian(key_list[7], (ATOM_ROWS, ATOM_COLS, ORBITALS, VECTORS), 1.0, 6.0, ((0, 16), (1, 48)), jnp.float32),
    }


OFFSETS = ((0, 1), (1, 0), (1, 1))
CENTRE = 4.0
HALF_WIDTH = 24.0


def shifted(values, row_step, col_step):
    return jnp.roll(values, (-row_step, -col_step), axis=(0, 1))


def contract(blocks, vectors_in):
    return jnp.einsum("xyab,xybv->xyav", blocks, vectors_in, precision=lax.Precision.HIGHEST)


def reference(features, pair_mask, w_update, w_atom, w_pair, slot_bias, w_block, trial):
    height, breadth = features.shape[0], features.shape[1]
    widened = features.astype(jnp.float32)
    gathered = jnp.zeros_like(widened)
    for row_step, col_step in OFFSETS:
        gathered = gathered + shifted(widened, row_step, col_step) + shifted(widened, -row_step, -col_step)
    update = jax.nn.silu(jnp.dot(gathered.astype(jnp.bfloat16), w_update, preferred_element_type=jnp.float32))
    refined = (widened + update).astype(jnp.bfloat16)
    self_part = jnp.dot(refined, w_atom, preferred_element_type=jnp.float32)
    pair_part = jnp.dot(features, w_pair, preferred_element_type=jnp.float32)
    forward = []
    for slot in range(3):
        row_step, col_step = OFFSETS[slot]
        message = jax.nn.silu(self_part + shifted(pair_part, row_step, col_step) + slot_bias[slot]).astype(jnp.bfloat16)
        predicted = jnp.dot(message, w_block, preferred_element_type=jnp.float32)
        predicted = predicted * pair_mask[:, :, slot:slot + 1].astype(jnp.float32)
        forward.append(predicted.reshape(height, breadth, ORBITALS, ORBITALS))
    message = jax.nn.silu(self_part + pair_part + slot_bias[3]).astype(jnp.bfloat16)
    predicted = jnp.dot(message, w_block, preferred_element_type=jnp.float32).reshape(height, breadth, ORBITALS, ORBITALS)
    onsite = 0.5 * (predicted + jnp.swapaxes(predicted, -1, -2))

    def operate(vectors_in):
        summed = contract(onsite, vectors_in)
        for slot in range(3):
            row_step, col_step = OFFSETS[slot]
            summed = summed + contract(forward[slot], shifted(vectors_in, row_step, col_step))
            backward = contract(jnp.swapaxes(forward[slot], -1, -2), vectors_in)
            summed = summed + shifted(backward, -row_step, -col_step)
        return summed

    def scaled(vectors_in):
        return (operate(vectors_in) - CENTRE * vectors_in) / HALF_WIDTH

    def chebyshev(start):
        before = start
        current = scaled(start)
        for turn in range(STEPS - 1):
            following = 2.0 * scaled(current) - before
            before, current = current, following
        return current

    width = trial.shape[3] // 4
    groups = trial.reshape(height, breadth, ORBITALS, 4, width).transpose(3, 0, 1, 2, 4)
    results = lax.map(chebyshev, groups)
    return results.transpose(1, 2, 3, 0, 4).reshape(height, breadth, ORBITALS, 4 * width)
```

```python
import functools

import jax
import jax.numpy as jnp
from jax import lax
from jax.experimental import pallas as pl
from jax.experimental.pallas import tpu as pltpu
from jax.sharding import PartitionSpec as P

ORBITALS = 13
PAD = 16
CENTRE = 4.0
HALF_WIDTH = 24.0
MESH = pl.DeviceIdType.MESH
F32 = jnp.float32
BF16 = jnp.bfloat16

SIDES = ((0, 1), (1, 1), (-1, 1), (0, -1), (-1, -1), (1, -1), (1, 0), (-1, 0))
BLOCKS = (
    (-1, -1, 0, 2, True),
    (-1, 0, 1, 1, True),
    (0, -1, 5, 0, True),
    (0, 0, 6, 3, False),
    (0, 1, 7, 0, False),
    (1, 0, 11, 1, False),
    (1, 1, 12, 2, False),
)


def span(step, size, width):
    if step > 0:
        return slice(size - width, size), slice(3 - width, 3)
    if step < 0:
        return slice(0, width), slice(3 + size, 3 + size + width)
    return slice(0, size), slice(3, 3 + size)


def iota(shape, axis):
    return lax.broadcasted_iota(jnp.int32, shape, axis)


def place_weights(w_block, base, transposed):
    lane = iota((ORBITALS * ORBITALS, 256), 1)
    source = iota((ORBITALS * ORBITALS, 256), 0)
    b = lane & 15
    a = 8 * (lane >> 7) + ((base - ((lane >> 4) & 7)) & 7)
    entry = b * ORBITALS + a if transposed else a * ORBITALS + b
    chosen = (source == entry) & (a < ORBITALS) & (b < ORBITALS)
    return jnp.dot(w_block, chosen.astype(F32).astype(BF16), preferred_element_type=F32).astype(BF16)


def kernel(
    features_hbm, mask_hbm, update_hbm, atom_hbm, pair_hbm, bias_hbm, block_hbm, trial_hbm,
    out_ref,
    features_in, mask_in, w_update, w_atom, w_pair, bias, w_block, trial,
    patches, mask_wide, x_hi, x_lo, y_hi, z_hi, y, z, placed, gather, select,
    self_part, pair_part, masks, blocks, h_full, h_hi, h_lo,
    load_sem, send_f, recv_f, send_x, recv_x,
):
    px, py = lax.axis_index("px"), lax.axis_index("py")
    nx, ny = lax.axis_size("px"), lax.axis_size("py")

    def device(side):
        return (lax.rem(px + side[0] + nx, nx), lax.rem(py + side[1] + ny, ny))

    barrier = pltpu.get_barrier_semaphore()
    for side in SIDES:
        pl.semaphore_signal(barrier, inc=1, device_id=device(side), device_id_type=MESH)

    loads = []
    pairs = (
        (trial_hbm, trial), (features_hbm, features_in), (mask_hbm, mask_in), (update_hbm, w_update),
        (atom_hbm, w_atom), (pair_hbm, w_pair), (bias_hbm, bias), (block_hbm, w_block),
    )
    for i, (source, target) in enumerate(pairs):
        copy = pltpu.make_async_copy(source, target, load_sem.at[i])
        copy.start()
        loads.append(copy)

    for rows, columns in ((0, slice(11, 14)), (slice(1, 3), 13), (9, slice(0, 3)), (slice(7, 9), 0)):
        x_hi[rows, columns] = jnp.zeros_like(x_hi[rows, columns])
    x_lo[...] = jnp.zeros_like(x_lo)
    mask_wide[...] = jnp.zeros_like(mask_wide)
    trial_pad = jnp.zeros((8, PAD - ORBITALS, 256), F32)
    for i in range(1, 3):
        loads[i].wait()
    patches[4, :, :128] = features_in[...].astype(F32).reshape(32, 128).astype(BF16)
    mask_wide[:, :3] = mask_in[...].astype(F32).reshape(32, 3)
    patches[4, :, 128:] = mask_wide[...].astype(BF16)
    loads[0].wait()
    for r in range(4):
        wide = jnp.concatenate([trial[r], trial_pad], axis=1)
        high = wide.astype(BF16)
        x_hi[3 + r, 3:11] = high
        x_lo[3 + r, 3:11] = (wide - high.astype(F32)).astype(BF16)

    pl.semaphore_wait(barrier, len(SIDES))

    feature_copies, vector_copies = [], []
    for i, side in enumerate(SIDES):
        mine = (1 - side[0]) * 3 + (1 - side[1])
        copy = pltpu.make_async_remote_copy(
            src_ref=patches.at[4], dst_ref=patches.at[mine], send_sem=send_f.at[i], recv_sem=recv_f.at[i],
            device_id=device(side), device_id_type=MESH,
        )
        copy.start()
        feature_copies.append(copy)
    for i, side in enumerate(SIDES):
        width = 2 if side[0] * side[1] < 0 else 3
        from_r, to_r = span(side[0], 4, width)
        from_c, to_c = span(side[1], 8, width)
        shift = lambda s: slice(3 + s.start, 3 + s.stop)
        copy = pltpu.make_async_remote_copy(
            src_ref=x_hi.at[shift(from_r), shift(from_c)], dst_ref=x_hi.at[to_r, to_c],
            send_sem=send_x.at[i], recv_sem=recv_x.at[i], device_id=device(side), device_id_type=MESH,
        )
        copy.start()
        vector_copies.append(copy)

    for i in range(3, 8):
        loads[i].wait()
    for i, (_, _, base, slot, transposed) in enumerate(BLOCKS):
        placed[i] = place_weights(w_block[...], base, transposed)
    placed[7] = place_weights(w_block[...], BLOCKS[3][2], True)
    y_hi[...] = jnp.zeros_like(y_hi)
    z_hi[...] = jnp.zeros_like(z_hi)
    h_full[...] = jnp.zeros_like(h_full)
    point = iota((224, 1), 0)
    cell = iota((1, 288), 1)
    patch = cell >> 5
    patch_row = (patch >= 3).astype(jnp.int32) + (patch >= 6).astype(jnp.int32)
    down = (patch_row * 4 - 4 + ((cell >> 3) & 3)) - ((point & 15) - 3)
    right = ((patch - 3 * patch_row) * 8 - 8 + (cell & 7)) - ((point >> 4) - 3)
    same = (down == 0) & (right == 0)
    near = (jnp.abs(down) <= 1) & (jnp.abs(right) <= 1) & (down + right != 0) | (
        (down == right) & (jnp.abs(down) == 1)
    )
    select[...] = same.astype(F32).astype(BF16)
    gather[...] = near.astype(F32).astype(BF16)

    for copy in feature_copies:
        copy.wait_recv()

    around = patches[...].reshape(288, 256)
    picked = jnp.dot(select[...], around, preferred_element_type=F32)
    gathered = jnp.dot(gather[...], around[:, :128], preferred_element_type=F32)
    own = picked[:, :128]
    update = jax.nn.silu(jnp.dot(gathered.astype(BF16), w_update[...], preferred_element_type=F32))
    refined = (own + update).astype(BF16)
    self_part[...] = jnp.dot(refined, w_atom[...], preferred_element_type=F32).reshape(14, 16, 128)
    pair_part[...] = jnp.dot(own.astype(BF16), w_pair[...], preferred_element_type=F32).reshape(14, 16, 128)
    masks[...] = picked[:, 128:].reshape(14, 16, 128)

    for i, (dr, dc, base, slot, transposed) in enumerate(BLOCKS):
        r0, c0 = (1 + dr, 1 + dc) if transposed else (1, 1)
        r1, c1 = (1, 1) if transposed else (1 + dr, 1 + dc)
        message = jax.nn.silu(
            self_part[c0 : c0 + 12, r0 : r0 + 8] + pair_part[c1 : c1 + 12, r1 : r1 + 8] + bias[slot : slot + 1]
        )
        if slot < 3:
            message = message * masks[c0 : c0 + 12, r0 : r0 + 8, slot : slot + 1]
        message = message.astype(BF16).reshape(96, 128)
        block = jnp.dot(message, placed[i], preferred_element_type=F32)
        if slot == 3:
            block = 0.5 * (block + jnp.dot(message, placed[7], preferred_element_type=F32))
        blocks[i] = block.reshape(12, 8, 256)

    lane_slot = iota((8, 128), 1) >> 4

    def assemble(g, carry):
        for c in range(4):
            for a in range(ORBITALS):
                half = slice(128 * (a // 8), 128 * (a // 8) + 128)
                for part in range(2):
                    value = jnp.zeros((8, 128), F32)
                    for i, (_, _, base, _, _) in enumerate(BLOCKS):
                        if (base + c) // 8 == part:
                            value = jnp.where(lane_slot == (base - a) % 8, blocks[i, g * 4 + c, :, half], value)
                    turn = (c + a) * 16 % 128
                    if turn:
                        value = pltpu.roll(value, turn, axis=1)
                    h_full[part, pl.ds(g * 64 + c * 16 + a, 8, stride=192), :] = value
        return carry

    lax.fori_loop(0, 3, assemble, 0)

    def halves(r, carry):
        rows = pl.ds(pl.multiple_of(r * 192, 192), 192)
        full = jnp.concatenate([h_full[0, rows, :], h_full[1, rows, :]], axis=1)
        high = full.astype(BF16)
        h_hi[rows, :] = high
        h_lo[rows, :] = (full - high.astype(F32)).astype(BF16)
        return carry

    lax.fori_loop(0, 8, halves, 0)

    for copy in vector_copies:
        copy.wait_recv()

    def apply(vectors, r, g, first, last):
        c = 1 + 4 * g
        weights = jnp.concatenate(
            [
                vectors[r, c - 1 : c + 4].reshape(80, 256),
                vectors[r + 1, c - 1 : c + 5].reshape(96, 256),
                vectors[r + 2, c : c + 5].reshape(80, 256),
            ],
            axis=0,
        )
        rows = pl.ds(pl.multiple_of(r * 192 + g * 64 + first * 16, 16), (last - first) * 16)
        total = jnp.dot(h_hi[rows, :], weights, preferred_element_type=F32)
        total = total + jnp.dot(h_lo[rows, :], weights, preferred_element_type=F32)
        return total.reshape(last - first, PAD, 256)

    def start(r, c, n):
        return x_hi[r, c : c + n].astype(F32) + x_lo[r, c : c + n].astype(F32)

    def first_step(r, carry):
        for g in range(3):
            c = 1 + 4 * g
            value = (apply(x_hi, r, g, 0, 4) - CENTRE * start(r + 1, c, 4)) * (1.0 / HALF_WIDTH)
            y[r + 1, c : c + 4] = value
            y_hi[r + 1, c : c + 4] = value.astype(BF16)
        return carry

    lax.fori_loop(0, 8, first_step, 0)

    def second_step(r, carry):
        for g in range(3):
            c = 1 + 4 * g
            value = (apply(y_hi, r, g, 0, 4) - CENTRE * y[r + 1, c : c + 4]) * (2.0 / HALF_WIDTH)
            value = value - start(r + 1, c, 4)
            z_hi[r + 1, c : c + 4] = value.astype(BF16)
            z[r + 1, c : c + 4] = value
        return carry

    lax.fori_loop(1, 7, second_step, 0)

    def third_step(r, carry):
        for g, first, last in ((0, 2, 4), (1, 0, 4), (2, 0, 2)):
            c, n = 1 + 4 * g + first, last - first
            value = (apply(z_hi, r, g, first, last) - CENTRE * z[r + 1, c : c + n]) * (2.0 / HALF_WIDTH)
            value = value - y[r + 1, c : c + n]
            out_ref[r - 2, c - 3 : c - 3 + n] = value[:, :ORBITALS]
        return carry

    lax.fori_loop(2, 6, third_step, 0)

    for copy in feature_copies + vector_copies:
        copy.wait_send()


def per_device(features, pair_mask, w_update, w_atom, w_pair, slot_bias, w_block, trial):
    vectors = (10, 14, PAD, 256)
    sides = pltpu.SemaphoreType.DMA((len(SIDES),))
    return pl.pallas_call(
        kernel,
        name="filter",
        out_shape=jax.ShapeDtypeStruct(trial.shape, trial.dtype),
        in_specs=[pl.BlockSpec(memory_space=pl.ANY)] * 8,
        out_specs=pl.BlockSpec(memory_space=pltpu.VMEM),
        scratch_shapes=[
            pltpu.VMEM(features.shape, BF16),
            pltpu.VMEM(pair_mask.shape, jnp.int32),
            pltpu.VMEM(w_update.shape, BF16),
            pltpu.VMEM(w_atom.shape, BF16),
            pltpu.VMEM(w_pair.shape, BF16),
            pltpu.VMEM(slot_bias.shape, F32),
            pltpu.VMEM(w_block.shape, BF16),
            pltpu.VMEM(trial.shape, F32),
            pltpu.VMEM((9, 32, 256), BF16),
            pltpu.VMEM((32, 128), F32),
            pltpu.VMEM(vectors, BF16),
            pltpu.VMEM(vectors, BF16),
            pltpu.VMEM(vectors, BF16),
            pltpu.VMEM(vectors, BF16),
            pltpu.VMEM(vectors, F32),
            pltpu.VMEM(vectors, F32),
            pltpu.VMEM((8, 128, 256), BF16),
            pltpu.VMEM((224, 288), BF16),
            pltpu.VMEM((224, 288), BF16),
            pltpu.VMEM((14, 16, 128), F32),
            pltpu.VMEM((14, 16, 128), F32),
            pltpu.VMEM((14, 16, 128), F32),
            pltpu.VMEM((7, 12, 8, 256), F32),
            pltpu.VMEM((2, 1536, 128), F32),
            pltpu.VMEM((1536, 256), BF16),
            pltpu.VMEM((1536, 256), BF16),
            pltpu.SemaphoreType.DMA((8,)),
            sides,
            sides,
            sides,
            sides,
        ],
        compiler_params=pltpu.CompilerParams(
            collective_id=0, has_side_effects=True, vmem_limit_bytes=48 * 2**20
        ),
    )(features, pair_mask, w_update, w_atom, w_pair, slot_bias, w_block, trial)


def solution(mesh):
    return jax.shard_map(
        per_device,
        mesh=mesh,
        in_specs=(
            P("px", "py", None),
            P("px", "py", None),
            P(),
            P(),
            P(),
            P(),
            P(),
            P("px", "py", None, None),
        ),
        out_specs=P("px", "py", None, None),
        check_vma=False,
    )
```

```python
import functools

import jax
import jax.numpy as jnp
from jax import lax
from jax.experimental import pallas as pl
from jax.experimental.pallas import tpu as pltpu
from jax.sharding import PartitionSpec as P

ORBITALS = 13
PAD = 16
CENTRE = 4.0
HALF_WIDTH = 24.0
MESH = pl.DeviceIdType.MESH
F32 = jnp.float32
BF16 = jnp.bfloat16

FORWARD = ((0, 1), (1, 1), (-1, 1))
BACKWARD = ((0, -1), (-1, -1), (1, -1))
ACROSS = ((1, 0), (-1, 0))
SIDES = FORWARD + BACKWARD + ACROSS
LAYERS = 12
BLOCKS = (
    (-1, -1, 0, 2, True),
    (-1, 0, 1, 1, True),
    (0, -1, 5, 0, True),
    (0, 0, 6, 3, False),
    (0, 1, 7, 0, False),
    (1, 0, 11, 1, False),
    (1, 1, 12, 2, False),
)


def span(step, size, width):
    if step > 0:
        return slice(size - width, size), slice(3 - width, 3)
    if step < 0:
        return slice(0, width), slice(3 + size, 3 + size + width)
    return slice(0, size), slice(3, 3 + size)


def iota(shape, axis):
    return lax.broadcasted_iota(jnp.int32, shape, axis)


def place_weights(w_block, base, transposed):
    lane = iota((ORBITALS * ORBITALS, 256), 1)
    source = iota((ORBITALS * ORBITALS, 256), 0)
    b = lane & 15
    a = 8 * (lane >> 7) + ((base - ((lane >> 4) & 7)) & 7)
    entry = b * ORBITALS + a if transposed else a * ORBITALS + b
    chosen = (source == entry) & (a < ORBITALS) & (b < ORBITALS)
    return lax.dot_general(
        w_block, chosen.astype(F32).astype(BF16), (((0,), (0,)), ((), ())), preferred_element_type=F32
    ).astype(BF16)


def kernel(
    features_hbm, mask_hbm, update_hbm, atom_hbm, pair_hbm, bias_hbm, block_hbm, trial_hbm,
    out_hbm,
    features_in, mask_in, w_update, w_atom, w_pair, bias, w_block, trial,
    patches, x_hi, x_lo, y_hi, z_hi, y, z, placed, gather, select,
    self_part, pair_part, masks, blocks, h_full, h_hi, h_lo, result,
    load_sem, out_sem, send_f, recv_f, send_x, recv_x,
):
    px, py = lax.axis_index("px"), lax.axis_index("py")
    nx, ny = lax.axis_size("px"), lax.axis_size("py")

    def device(side):
        return (lax.rem(px + side[0] + nx, nx), lax.rem(py + side[1] + ny, ny))

    inner = lax.rem(py, LAYERS) != LAYERS - 1

    def greet(sides):
        for side in sides:
            pl.semaphore_signal(barrier, inc=1, device_id=device(side), device_id_type=MESH)

    barrier = pltpu.get_barrier_semaphore()
    greet(BACKWARD)
    pl.when(inner)(lambda: greet(ACROSS))

    loads = []
    pairs = (
        (trial_hbm.at[:, :, :128], trial.at[0]), (trial_hbm.at[:, :, 128:], trial.at[1]),
        (features_hbm, features_in), (mask_hbm, mask_in), (update_hbm, w_update),
        (atom_hbm, w_atom), (pair_hbm, w_pair), (bias_hbm, bias), (block_hbm, w_block),
    )
    for i, (source, target) in enumerate(pairs):
        copy = pltpu.make_async_copy(source, target, load_sem.at[i])
        copy.start()
        loads.append(copy)

    for rows, columns in ((0, slice(11, 14)), (slice(1, 3), 13), (9, slice(0, 3)), (slice(7, 9), 0)):
        x_hi[rows, columns] = jnp.zeros_like(x_hi[rows, columns])
    x_lo[...] = jnp.zeros_like(x_lo)
    loads[2].wait()
    patches[4, :, :128] = features_in[...].astype(F32).reshape(32, 128).astype(BF16)
    loads[3].wait()
    row_of, column_of = iota((32, 8), 0), iota((32, 8), 1)
    spread = (column_of == (row_of & 7)).astype(F32)
    expand = (iota((32, 4), 1) == (iota((32, 4), 0) >> 3)).astype(BF16)
    wide = jnp.zeros((32, 128), F32)
    for k in range(3):
        by_row = jnp.dot(expand, mask_in[k].astype(F32).astype(BF16), preferred_element_type=F32)
        wide = wide + jnp.where(iota((32, 128), 1) == k, jnp.sum(by_row * spread, axis=1, keepdims=True), 0.0)
    patches[4, :, 128:] = wide.astype(BF16)
    loads[0].wait()
    loads[1].wait()
    trial_pad = jnp.zeros((PAD - ORBITALS, 256), F32)
    for r in range(4):
        for c in range(8):
            atom = jnp.concatenate([trial[h, r, pl.ds(c, ORBITALS, stride=8), :] for h in range(2)], axis=1)
            atom = jnp.concatenate([atom, trial_pad], axis=0)
            high = atom.astype(BF16)
            x_hi[3 + r, 3 + c] = high
            x_lo[3 + r, 3 + c] = (atom - high.astype(F32)).astype(BF16)

    feature_copies, vector_copies = {}, {}
    for i, side in enumerate(SIDES):
        mine = (1 - side[0]) * 3 + (1 - side[1])
        feature_copies[side] = pltpu.make_async_remote_copy(
            src_ref=patches.at[4], dst_ref=patches.at[mine], send_sem=send_f.at[i], recv_sem=recv_f.at[i],
            device_id=device(side), device_id_type=MESH,
        )
        width = 2 if side[0] * side[1] < 0 else 3
        from_r, to_r = span(side[0], 4, width)
        from_c, to_c = span(side[1], 8, width)
        shift = lambda s: slice(3 + s.start, 3 + s.stop)
        vector_copies[side] = pltpu.make_async_remote_copy(
            src_ref=x_hi.at[shift(from_r), shift(from_c)], dst_ref=x_hi.at[to_r, to_c],
            send_sem=send_x.at[i], recv_sem=recv_x.at[i], device_id=device(side), device_id_type=MESH,
        )

    def send(sides):
        for side in sides:
            feature_copies[side].start()
        for side in sides:
            vector_copies[side].start()

    pl.semaphore_wait(barrier, jnp.where(inner, len(FORWARD) + len(ACROSS), len(FORWARD)))
    send(FORWARD)
    pl.when(inner)(lambda: send(ACROSS))

    for i in range(4, 9):
        loads[i].wait()
    for i, (_, _, base, slot, transposed) in enumerate(BLOCKS):
        placed[i] = place_weights(w_block[...], base, transposed)
    placed[7] = place_weights(w_block[...], BLOCKS[3][2], True)
    y_hi[...] = jnp.zeros_like(y_hi)
    z_hi[...] = jnp.zeros_like(z_hi)
    h_full[...] = jnp.zeros_like(h_full)
    point = iota((224, 1), 0)
    cell = iota((1, 288), 1)
    patch = cell >> 5
    patch_row = (patch >= 3).astype(jnp.int32) + (patch >= 6).astype(jnp.int32)
    down = (patch_row * 4 - 4 + ((cell >> 3) & 3)) - ((point & 15) - 3)
    right = ((patch - 3 * patch_row) * 8 - 8 + (cell & 7)) - ((point >> 4) - 3)
    same = (down == 0) & (right == 0)
    near = (jnp.abs(down) <= 1) & (jnp.abs(right) <= 1) & (down + right != 0) | (
        (down == right) & (jnp.abs(down) == 1)
    )
    select[...] = same.astype(F32).astype(BF16)
    gather[...] = near.astype(F32).astype(BF16)

    for side in FORWARD:
        feature_copies[side].wait_recv()
    send(BACKWARD)
    pl.when(jnp.logical_not(inner))(lambda: send(ACROSS))
    for side in BACKWARD + ACROSS:
        feature_copies[side].wait_recv()

    around = patches[...].reshape(288, 256)
    picked = jnp.dot(select[...], around, preferred_element_type=F32)
    gathered = jnp.dot(gather[...], around[:, :128], preferred_element_type=F32)
    own = picked[:, :128]
    update = jax.nn.silu(jnp.dot(gathered.astype(BF16), w_update[...], preferred_element_type=F32))
    refined = (own + update).astype(BF16)
    self_part[...] = jnp.dot(refined, w_atom[...], preferred_element_type=F32).reshape(14, 16, 128)
    pair_part[...] = jnp.dot(own.astype(BF16), w_pair[...], preferred_element_type=F32).reshape(14, 16, 128)
    masks[...] = picked[:, 128:].reshape(14, 16, 128)

    for i, (dr, dc, base, slot, transposed) in enumerate(BLOCKS):
        r0, c0 = (1 + dr, 1 + dc) if transposed else (1, 1)
        r1, c1 = (1, 1) if transposed else (1 + dr, 1 + dc)
        message = jax.nn.silu(
            self_part[c0 : c0 + 12, r0 : r0 + 8] + pair_part[c1 : c1 + 12, r1 : r1 + 8] + bias[slot : slot + 1]
        )
        if slot < 3:
            message = message * masks[c0 : c0 + 12, r0 : r0 + 8, slot : slot + 1]
        message = message.astype(BF16).reshape(96, 128)
        block = jnp.dot(message, placed[i], preferred_element_type=F32)
        if slot == 3:
            block = 0.5 * (block + jnp.dot(message, placed[7], preferred_element_type=F32))
        blocks[i] = block.reshape(12, 8, 256)

    lane_slot = iota((8, 128), 1) >> 4

    def assemble(g, carry):
        for c in range(4):
            for a in range(ORBITALS):
                half = slice(128 * (a // 8), 128 * (a // 8) + 128)
                for part in range(2):
                    value = jnp.zeros((8, 128), F32)
                    for i, (_, _, base, _, _) in enumerate(BLOCKS):
                        if (base + c) // 8 == part:
                            value = jnp.where(lane_slot == (base - a) % 8, blocks[i, g * 4 + c, :, half], value)
                    turn = (c + a) * 16 % 128
                    if turn:
                        value = pltpu.roll(value, turn, axis=1)
                    h_full[part, pl.ds(g * 64 + c * 16 + a, 8, stride=192), :] = value
        return carry

    lax.fori_loop(0, 3, assemble, 0)

    def halves(r, carry):
        rows = pl.ds(pl.multiple_of(r * 192, 192), 192)
        full = jnp.concatenate([h_full[0, rows, :], h_full[1, rows, :]], axis=1)
        high = full.astype(BF16)
        h_hi[rows, :] = high
        h_lo[rows, :] = (full - high.astype(F32)).astype(BF16)
        return carry

    lax.fori_loop(0, 8, halves, 0)

    for side in SIDES:
        vector_copies[side].wait_recv()

    def apply(vectors, r, g, first, last):
        c = 1 + 4 * g
        weights = jnp.concatenate(
            [
                vectors[r, c - 1 : c + 4].reshape(80, 256),
                vectors[r + 1, c - 1 : c + 5].reshape(96, 256),
                vectors[r + 2, c : c + 5].reshape(80, 256),
            ],
            axis=0,
        )
        rows = pl.ds(pl.multiple_of(r * 192 + g * 64 + first * 16, 16), (last - first) * 16)
        total = jnp.dot(h_hi[rows, :], weights, preferred_element_type=F32)
        total = total + jnp.dot(h_lo[rows, :], weights, preferred_element_type=F32)
        return total.reshape(last - first, PAD, 256)

    def start(r, c, n):
        return x_hi[r, c : c + n].astype(F32) + x_lo[r, c : c + n].astype(F32)

    def first_step(r, carry):
        for g in range(3):
            c = 1 + 4 * g
            value = (apply(x_hi, r, g, 0, 4) - CENTRE * start(r + 1, c, 4)) * (1.0 / HALF_WIDTH)
            y[r + 1, c : c + 4] = value
            y_hi[r + 1, c : c + 4] = value.astype(BF16)
        return carry

    lax.fori_loop(0, 8, first_step, 0)

    def second_step(r, carry):
        for g in range(3):
            c = 1 + 4 * g
            value = (apply(y_hi, r, g, 0, 4) - CENTRE * y[r + 1, c : c + 4]) * (2.0 / HALF_WIDTH)
            value = value - start(r + 1, c, 4)
            z_hi[r + 1, c : c + 4] = value.astype(BF16)
            z[r + 1, c : c + 4] = value
        return carry

    lax.fori_loop(1, 7, second_step, 0)

    def third_step(r, carry):
        for g, first, last in ((0, 2, 4), (1, 0, 4), (2, 0, 2)):
            c, n = 1 + 4 * g + first, last - first
            value = (apply(z_hi, r, g, first, last) - CENTRE * z[r + 1, c : c + n]) * (2.0 / HALF_WIDTH)
            value = value - y[r + 1, c : c + n]
            for h in range(2):
                for k in range(n):
                    result[h, r - 2, pl.ds(c - 3 + k, ORBITALS, stride=8), :] = value[
                        k, :ORBITALS, 128 * h : 128 * h + 128
                    ]
        for h in range(2):
            out_copy(r - 2, h).start()
        return carry

    def out_copy(r, h):
        return pltpu.make_async_copy(
            result.at[h, r], out_hbm.at[r, :, 128 * h : 128 * h + 128], out_sem.at[h, r]
        )

    lax.fori_loop(2, 6, third_step, 0)

    for side in SIDES:
        feature_copies[side].wait_send()
        vector_copies[side].wait_send()
    for r in range(4):
        for h in range(2):
            out_copy(r, h).wait()


def per_device(features, pair_mask, w_update, w_atom, w_pair, slot_bias, w_block, trial):
    pair_mask = pair_mask.transpose(2, 0, 1)
    w_block = w_block.T
    rows, columns, _, width = trial.shape
    trial = trial.transpose(0, 2, 1, 3).reshape(rows, ORBITALS * columns, width)
    halves = (2, rows, ORBITALS * columns, 128)
    vectors = (10, 14, PAD, 256)
    sides = pltpu.SemaphoreType.DMA((len(SIDES),))
    filtered = pl.pallas_call(
        kernel,
        name="filter",
        out_shape=jax.ShapeDtypeStruct(trial.shape, trial.dtype),
        in_specs=[pl.BlockSpec(memory_space=pl.ANY)] * 8,
        out_specs=pl.BlockSpec(memory_space=pl.ANY),
        scratch_shapes=[
            pltpu.VMEM(features.shape, BF16),
            pltpu.VMEM(pair_mask.shape, jnp.int32),
            pltpu.VMEM(w_update.shape, BF16),
            pltpu.VMEM(w_atom.shape, BF16),
            pltpu.VMEM(w_pair.shape, BF16),
            pltpu.VMEM(slot_bias.shape, F32),
            pltpu.VMEM(w_block.shape, BF16),
            pltpu.VMEM(halves, F32),
            pltpu.VMEM((9, 32, 256), BF16),
            pltpu.VMEM(vectors, BF16),
            pltpu.VMEM(vectors, BF16),
            pltpu.VMEM(vectors, BF16),
            pltpu.VMEM(vectors, BF16),
            pltpu.VMEM(vectors, F32),
            pltpu.VMEM(vectors, F32),
            pltpu.VMEM((8, 128, 256), BF16),
            pltpu.VMEM((224, 288), BF16),
            pltpu.VMEM((224, 288), BF16),
            pltpu.VMEM((14, 16, 128), F32),
            pltpu.VMEM((14, 16, 128), F32),
            pltpu.VMEM((14, 16, 128), F32),
            pltpu.VMEM((7, 12, 8, 256), F32),
            pltpu.VMEM((2, 1536, 128), F32),
            pltpu.VMEM((1536, 256), BF16),
            pltpu.VMEM((1536, 256), BF16),
            pltpu.VMEM(halves, F32),
            pltpu.SemaphoreType.DMA((9,)),
            pltpu.SemaphoreType.DMA((2, 4)),
            sides,
            sides,
            sides,
            sides,
        ],
        compiler_params=pltpu.CompilerParams(
            collective_id=0, has_side_effects=True, vmem_limit_bytes=60 * 2**20
        ),
    )(features, pair_mask, w_update, w_atom, w_pair, slot_bias, w_block, trial)
    return filtered.reshape(rows, ORBITALS, columns, width).transpose(0, 2, 1, 3)


def solution(mesh):
    return jax.shard_map(
        per_device,
        mesh=mesh,
        in_specs=(
            P("px", "py", None),
            P("px", "py", None),
            P(),
            P(),
            P(),
            P(),
            P(),
            P("px", "py", None, None),
        ),
        out_specs=P("px", "py", None, None),
        check_vma=False,
    )
```

```python
import functools

import jax
import jax.numpy as jnp
from jax import lax
from jax.experimental import pallas as pl
from jax.experimental.pallas import tpu as pltpu
from jax.sharding import PartitionSpec as P

ORBITALS = 13
PAD = 16
CENTRE = 4.0
HALF_WIDTH = 24.0
MESH = pl.DeviceIdType.MESH
F32 = jnp.float32
BF16 = jnp.bfloat16

FORWARD = ((0, 1), (1, 1), (-1, 1))
BACKWARD = ((0, -1), (-1, -1), (1, -1))
ACROSS = ((1, 0), (-1, 0))
SIDES = FORWARD + BACKWARD + ACROSS
LAYERS = 12
UNROLL = True
BLOCKS = (
    (-1, -1, 0, 2, True),
    (-1, 0, 1, 1, True),
    (0, -1, 5, 0, True),
    (0, 0, 6, 3, False),
    (0, 1, 7, 0, False),
    (1, 0, 11, 1, False),
    (1, 1, 12, 2, False),
)


def span(step, size, width):
    if step > 0:
        return slice(size - width, size), slice(3 - width, 3)
    if step < 0:
        return slice(0, width), slice(3 + size, 3 + size + width)
    return slice(0, size), slice(3, 3 + size)


def iota(shape, axis):
    return lax.broadcasted_iota(jnp.int32, shape, axis)


def place_weights(w_block, base, transposed):
    lane = iota((ORBITALS * ORBITALS, 256), 1)
    source = iota((ORBITALS * ORBITALS, 256), 0)
    b = lane & 15
    a = 8 * (lane >> 7) + ((base - ((lane >> 4) & 7)) & 7)
    entry = b * ORBITALS + a if transposed else a * ORBITALS + b
    chosen = (source == entry) & (a < ORBITALS) & (b < ORBITALS)
    return lax.dot_general(
        w_block, chosen.astype(F32).astype(BF16), (((0,), (0,)), ((), ())), preferred_element_type=F32
    ).astype(BF16)


def kernel(
    features_hbm, mask_hbm, update_hbm, atom_hbm, pair_hbm, bias_hbm, block_hbm, trial_hbm,
    out_ref,
    features_in, mask_in, w_update, w_atom, w_pair, bias, w_block, trial,
    patches, x_hi, x_lo, y_hi, z_hi, y, z, placed, gather, select,
    self_part, pair_part, masks, blocks, h_full, h,
    load_sem, send_f, recv_f, send_x, recv_x,
):
    px, py = lax.axis_index("px"), lax.axis_index("py")
    nx, ny = lax.axis_size("px"), lax.axis_size("py")

    def device(side):
        return (lax.rem(px + side[0] + nx, nx), lax.rem(py + side[1] + ny, ny))

    layer = lax.rem(py, LAYERS)
    first, last = layer == 0, layer == LAYERS - 1

    def greet(sides):
        for side in sides:
            pl.semaphore_signal(barrier, inc=1, device_id=device(side), device_id_type=MESH)

    barrier = pltpu.get_barrier_semaphore()
    greet(BACKWARD)
    pl.when(jnp.logical_not(last))(lambda: greet(ACROSS))
    pl.when(layer < LAYERS - 2)(lambda: greet(FORWARD))

    loads = []
    pairs = (
        (trial_hbm.at[:, :, :128], trial.at[0]), (trial_hbm.at[:, :, 128:], trial.at[1]),
        (features_hbm, features_in), (mask_hbm, mask_in), (update_hbm, w_update),
        (atom_hbm, w_atom), (pair_hbm, w_pair), (bias_hbm, bias), (block_hbm, w_block),
    )
    for i, (source, target) in enumerate(pairs):
        copy = pltpu.make_async_copy(source, target, load_sem.at[i])
        copy.start()
        loads.append(copy)

    for rows, columns in ((0, slice(11, 14)), (slice(1, 3), 13), (9, slice(0, 3)), (slice(7, 9), 0)):
        x_hi[rows, columns] = jnp.zeros_like(x_hi[rows, columns])
    x_lo[...] = jnp.zeros_like(x_lo)
    loads[2].wait()
    patches[4, :, :128] = features_in[...].astype(F32).reshape(32, 128).astype(BF16)
    loads[3].wait()
    row_of, column_of = iota((32, 8), 0), iota((32, 8), 1)
    spread = (column_of == (row_of & 7)).astype(F32)
    expand = (iota((32, 4), 1) == (iota((32, 4), 0) >> 3)).astype(BF16)
    wide = jnp.zeros((32, 128), F32)
    for k in range(3):
        by_row = jnp.dot(expand, mask_in[k].astype(F32).astype(BF16), preferred_element_type=F32)
        wide = wide + jnp.where(iota((32, 128), 1) == k, jnp.sum(by_row * spread, axis=1, keepdims=True), 0.0)
    patches[4, :, 128:] = wide.astype(BF16)
    loads[0].wait()
    loads[1].wait()
    trial_pad = jnp.zeros((PAD - ORBITALS, 256), F32)
    for r in range(4):
        for c in range(8):
            atom = jnp.concatenate([trial[h, r, pl.ds(c, ORBITALS, stride=8), :] for h in range(2)], axis=1)
            atom = jnp.concatenate([atom, trial_pad], axis=0)
            high = atom.astype(BF16)
            x_hi[3 + r, 3 + c] = high
            x_lo[3 + r, 3 + c] = (atom - high.astype(F32)).astype(BF16)

    feature_copies, vector_copies = {}, {}
    for i, side in enumerate(SIDES):
        mine = (1 - side[1]) * 3 + (1 - side[0])
        feature_copies[side] = pltpu.make_async_remote_copy(
            src_ref=patches.at[4], dst_ref=patches.at[mine], send_sem=send_f.at[i], recv_sem=recv_f.at[i],
            device_id=device(side), device_id_type=MESH,
        )
        width = 2 if side[0] * side[1] < 0 else 3
        from_r, to_r = span(side[0], 4, width)
        from_c, to_c = span(side[1], 8, width)
        shift = lambda s: slice(3 + s.start, 3 + s.stop)
        vector_copies[side] = pltpu.make_async_remote_copy(
            src_ref=x_hi.at[shift(from_r), shift(from_c)], dst_ref=x_hi.at[to_r, to_c],
            send_sem=send_x.at[i], recv_sem=recv_x.at[i], device_id=device(side), device_id_type=MESH,
        )

    def send(sides):
        for side in sides:
            feature_copies[side].start()
        for side in sides:
            vector_copies[side].start()

    pl.semaphore_wait(barrier, jnp.where(last, 3, jnp.where(first, 5, 8)))
    send(FORWARD)
    pl.when(jnp.logical_not(last))(lambda: send(ACROSS))
    pl.when(jnp.logical_not(first | last))(lambda: send(BACKWARD))

    for i in range(4, 9):
        loads[i].wait()
    for i, (_, _, base, slot, transposed) in enumerate(BLOCKS):
        placed[i] = place_weights(w_block[...], base, transposed)
    placed[7] = place_weights(w_block[...], BLOCKS[3][2], True)
    y_hi[...] = jnp.zeros_like(y_hi)
    z_hi[...] = jnp.zeros_like(z_hi)
    h_full[...] = jnp.zeros_like(h_full)

    point = iota((160, 1), 0)
    cell = iota((1, 192), 1)
    patch = cell >> 5
    patch_column = (patch >= 3).astype(jnp.int32)
    cell_row = (patch - 3 * patch_column) * 4 - 4 + ((cell >> 3) & 3)
    for i, (first_patch, first_point) in enumerate(((0, 1), (-8, -3))):
        down = cell_row - ((point & 15) - 3)
        right = (patch_column * 8 + first_patch + (cell & 7)) - ((point >> 4) + first_point)
        same = (down == 0) & (right == 0)
        near = (jnp.abs(down) <= 1) & (jnp.abs(right) <= 1) & (down + right != 0) | (
            (down == right) & (jnp.abs(down) == 1)
        )
        select[i] = same.astype(F32).astype(BF16)
        gather[i] = near.astype(F32).astype(BF16)

    lane_slot = iota((8, 128), 1) >> 4

    def build(left):
        i, columns = (1, 6) if left else (0, 10)
        atoms, wide = columns * 16, columns - 2
        around = (patches[:6] if left else patches[3:]).reshape(192, 256)
        picked = jnp.dot(select[i, :atoms], around, preferred_element_type=F32)
        gathered = jnp.dot(gather[i, :atoms], around[:, :128], preferred_element_type=F32)
        own = picked[:, :128]
        update = jax.nn.silu(jnp.dot(gathered.astype(BF16), w_update[...], preferred_element_type=F32))
        refined = (own + update).astype(BF16)
        shape = (columns, 16, 128)
        self_part[:columns] = jnp.dot(refined, w_atom[...], preferred_element_type=F32).reshape(shape)
        pair_part[:columns] = jnp.dot(own.astype(BF16), w_pair[...], preferred_element_type=F32).reshape(shape)
        masks[:columns] = picked[:, 128:].reshape(shape)

        for i, (dr, dc, _, slot, transposed) in enumerate(BLOCKS):
            r0, c0 = (1 + dr, 1 + dc) if transposed else (1, 1)
            r1, c1 = (1, 1) if transposed else (1 + dr, 1 + dc)
            message = jax.nn.silu(
                self_part[c0 : c0 + wide, r0 : r0 + 8]
                + pair_part[c1 : c1 + wide, r1 : r1 + 8]
                + bias[slot : slot + 1]
            )
            if slot < 3:
                message = message * masks[c0 : c0 + wide, r0 : r0 + 8, slot : slot + 1]
            message = message.astype(BF16).reshape(wide * 8, 128)
            block = jnp.dot(message, placed[i], preferred_element_type=F32)
            if slot == 3:
                block = 0.5 * (block + jnp.dot(message, placed[7], preferred_element_type=F32))
            blocks[i, :wide] = block.reshape(wide, 8, 256)

        for g in (0,) if left else (1, 2):
            for c in range(4):
                at = c + 4 * max(g - 1, 0)
                for a in range(ORBITALS):
                    half = slice(128 * (a // 8), 128 * (a // 8) + 128)
                    for part in range(2):
                        value = jnp.zeros((8, 128), F32)
                        for i, (_, _, base, _, _) in enumerate(BLOCKS):
                            if (base + c) // 8 == part:
                                value = jnp.where(lane_slot == (base - a) % 8, blocks[i, at, :, half], value)
                        turn = (c + a) * 16 % 128
                        if turn:
                            value = pltpu.roll(value, turn, axis=1)
                        h_full[g, part, pl.ds(c * 16 + a, 8, stride=64), :] = value

            def halves(r, carry):
                rows = pl.ds(pl.multiple_of(r * 64, 64), 64)
                full = jnp.concatenate([h_full[g, 0, rows, :], h_full[g, 1, rows, :]], axis=1)
                high = full.astype(BF16)
                h[g, r, :64] = high
                h[g, r, 64:] = (full - high.astype(F32)).astype(BF16)
                return carry

            lax.fori_loop(0, 8, halves, 0, unroll=UNROLL)

    def apply(vectors, r, g, begin=0, end=4):
        c = 1 + 4 * g
        weights = jnp.concatenate(
            [
                vectors[r, c - 1 : c + 4].reshape(80, 256),
                vectors[r + 1, c - 1 : c + 5].reshape(96, 256),
                vectors[r + 2, c : c + 5].reshape(80, 256),
            ],
            axis=0,
        )
        rows = slice(16 * begin, 16 * end)
        parts = jnp.concatenate([h[g, r, :64][rows], h[g, r, 64:][rows]], axis=0)
        total = jnp.dot(parts, weights, preferred_element_type=F32)
        size = 16 * (end - begin)
        return (total[:size] + total[size:]).reshape(end - begin, PAD, 256)

    def start(r, c, n):
        return x_hi[r, c : c + n].astype(F32) + x_lo[r, c : c + n].astype(F32)

    def first_step(groups):
        def row(r, carry):
            for g in groups:
                c = 1 + 4 * g
                value = (apply(x_hi, r, g) - CENTRE * start(r + 1, c, 4)) * (1.0 / HALF_WIDTH)
                y[r + 1, c : c + 4] = value
                y_hi[r + 1, c : c + 4] = value.astype(BF16)
            return carry

        lax.fori_loop(0, 8, row, 0, unroll=UNROLL)

    def second_step(groups):
        def row(r, carry):
            for g in groups:
                c = 1 + 4 * g
                value = (apply(y_hi, r, g) - CENTRE * y[r + 1, c : c + 4]) * (2.0 / HALF_WIDTH)
                value = value - start(r + 1, c, 4)
                z[r + 1, c : c + 4] = value
                z_hi[r + 1, c : c + 4] = value.astype(BF16)
            return carry

        lax.fori_loop(1, 7, row, 0, unroll=UNROLL)

    def third_row(r, carry):
        for g, begin, end in ((0, 2, 4), (1, 0, 4), (2, 0, 2)):
            c, n = 1 + 4 * g + begin, end - begin
            value = (apply(z_hi, r, g, begin, end) - CENTRE * z[r + 1, c : c + n]) * (2.0 / HALF_WIDTH)
            value = value - y[r + 1, c : c + n]
            for half in range(2):
                for k in range(n):
                    out_ref[pl.ds((r - 2) * 208 + half * 8 + c - 3 + k, ORBITALS, stride=16), :] = value[
                        k, :ORBITALS, 128 * half : 128 * half + 128
                    ]
        return carry

    def late():
        feature_copies[FORWARD[0]].wait_recv()
        pl.when(last)(lambda: send(ACROSS))
        for side in FORWARD[1:]:
            feature_copies[side].wait_recv()
        pl.when(first | last)(lambda: send(BACKWARD))

    pl.when(last)(late)
    for side in BACKWARD + ACROSS:
        feature_copies[side].wait_recv()
    build(left=False)
    for side in BACKWARD + ACROSS:
        vector_copies[side].wait_recv()
    first_step((1, 2))
    second_step((2,))

    pl.when(jnp.logical_not(last))(late)
    build(left=True)
    for side in FORWARD:
        vector_copies[side].wait_recv()
    first_step((0,))
    second_step((0, 1))
    lax.fori_loop(2, 6, third_row, 0, unroll=UNROLL)

    for side in SIDES:
        feature_copies[side].wait_send()
        vector_copies[side].wait_send()


def per_device(features, pair_mask, w_update, w_atom, w_pair, slot_bias, w_block, trial):
    pair_mask = pair_mask.transpose(2, 0, 1)
    w_block = w_block.T
    rows, columns, _, width = trial.shape
    trial = trial.transpose(0, 2, 1, 3).reshape(rows, ORBITALS * columns, width)
    halves = (2, rows, ORBITALS * columns, 128)
    vectors = (10, 14, PAD, 256)
    sides = pltpu.SemaphoreType.DMA((len(SIDES),))
    filtered = pl.pallas_call(
        kernel,
        name="filter",
        out_shape=jax.ShapeDtypeStruct((rows * ORBITALS * 2 * columns, 128), F32),
        in_specs=[pl.BlockSpec(memory_space=pltpu.HBM)] * 8,
        out_specs=pl.BlockSpec(memory_space=pltpu.VMEM),
        scratch_shapes=[
            pltpu.VMEM(features.shape, BF16),
            pltpu.VMEM(pair_mask.shape, jnp.int32),
            pltpu.VMEM(w_update.shape, BF16),
            pltpu.VMEM(w_atom.shape, BF16),
            pltpu.VMEM(w_pair.shape, BF16),
            pltpu.VMEM(slot_bias.shape, F32),
            pltpu.VMEM(w_block.shape, BF16),
            pltpu.VMEM(halves, F32),
            pltpu.VMEM((9, 32, 256), BF16),
            pltpu.VMEM(vectors, BF16),
            pltpu.VMEM(vectors, BF16),
            pltpu.VMEM(vectors, BF16),
            pltpu.VMEM(vectors, BF16),
            pltpu.VMEM(vectors, F32),
            pltpu.VMEM(vectors, F32),
            pltpu.VMEM((8, 128, 256), BF16),
            pltpu.VMEM((2, 160, 192), BF16),
            pltpu.VMEM((2, 160, 192), BF16),
            pltpu.VMEM((10, 16, 128), F32),
            pltpu.VMEM((10, 16, 128), F32),
            pltpu.VMEM((10, 16, 128), F32),
            pltpu.VMEM((7, 8, 8, 256), F32),
            pltpu.VMEM((3, 2, 512, 128), F32),
            pltpu.VMEM((3, 8, 128, 256), BF16),
            pltpu.SemaphoreType.DMA((9,)),
            sides,
            sides,
            sides,
            sides,
        ],
        compiler_params=pltpu.CompilerParams(
            collective_id=0, has_side_effects=True, vmem_limit_bytes=40 * 2**20
        ),
    )(
        *(
            pltpu.with_memory_space_constraint(array, pltpu.HBM)
            for array in (features, pair_mask, w_update, w_atom, w_pair, slot_bias, w_block, trial)
        )
    )
    filtered = filtered.reshape(rows, ORBITALS, 2, columns, 128).transpose(0, 1, 3, 2, 4)
    return filtered.reshape(rows, ORBITALS, columns, width).transpose(0, 2, 1, 3)


def solution(mesh):
    return jax.shard_map(
        per_device,
        mesh=mesh,
        in_specs=(
            P("px", "py", None),
            P("px", "py", None),
            P(),
            P(),
            P(),
            P(),
            P(),
            P("px", "py", None, None),
        ),
        out_specs=P("px", "py", None, None),
        check_vma=False,
    )
```

```python
import functools

import jax
import jax.numpy as jnp
from jax import lax
from jax.experimental import pallas as pl
from jax.experimental.pallas import tpu as pltpu
from jax.sharding import PartitionSpec as P

ORBITALS = 13
PAD = 16
CENTRE = 4.0
HALF_WIDTH = 24.0
MESH = pl.DeviceIdType.MESH
F32 = jnp.float32
BF16 = jnp.bfloat16

FORWARD = ((1, 1), (-1, 1), (0, 1))
BACKWARD = ((-1, -1), (1, -1), (0, -1))
ACROSS = ((1, 0), (-1, 0))
SIDES = FORWARD + BACKWARD + ACROSS
LAYERS = 12
UNROLL = True
BLOCKS = (
    (-1, -1, 0, 2, True),
    (-1, 0, 1, 1, True),
    (0, -1, 5, 0, True),
    (0, 0, 6, 3, False),
    (0, 1, 7, 0, False),
    (1, 0, 11, 1, False),
    (1, 1, 12, 2, False),
)


def span(step, size, width):
    if step > 0:
        return slice(size - width, size), slice(3 - width, 3)
    if step < 0:
        return slice(0, width), slice(3 + size, 3 + size + width)
    return slice(0, size), slice(3, 3 + size)


def iota(shape, axis):
    return lax.broadcasted_iota(jnp.int32, shape, axis)


def place_weights(w_block, base, transposed):
    lane = iota((ORBITALS * ORBITALS, 256), 1)
    source = iota((ORBITALS * ORBITALS, 256), 0)
    b = lane & 15
    a = 8 * (lane >> 7) + ((base - ((lane >> 4) & 7)) & 7)
    entry = b * ORBITALS + a if transposed else a * ORBITALS + b
    chosen = (source == entry) & (a < ORBITALS) & (b < ORBITALS)
    return lax.dot_general(
        w_block, chosen.astype(F32).astype(BF16), (((0,), (0,)), ((), ())), preferred_element_type=F32
    ).astype(BF16)


def kernel(
    features_hbm, mask_hbm, update_hbm, atom_hbm, pair_hbm, bias_hbm, block_hbm, trial_hbm,
    out_ref,
    features_in, mask_in, w_update, w_atom, w_pair, bias, w_block, trial,
    patches, x_hi, x_lo, y_hi, z_hi, y, z, placed, gather, select,
    self_part, pair_part, masks, blocks, h_full, h,
    load_sem, answered, send_f, recv_f, send_x, recv_x,
):
    px, py = lax.axis_index("px"), lax.axis_index("py")
    nx, ny = lax.axis_size("px"), lax.axis_size("py")

    def device(side):
        return (lax.rem(px + side[0] + nx, nx), lax.rem(py + side[1] + ny, ny))

    layer = lax.rem(py, LAYERS)
    first, last = layer == 0, layer == LAYERS - 1

    def greet(sides):
        for side in sides:
            pl.semaphore_signal(barrier, inc=1, device_id=device(side), device_id_type=MESH)

    barrier = pltpu.get_barrier_semaphore()
    pl.when(layer != 1)(lambda: greet(BACKWARD))
    pl.when(jnp.logical_not(last))(lambda: greet(ACROSS))
    pl.when(layer < LAYERS - 2)(lambda: greet(FORWARD))

    loads = []
    pairs = (
        (trial_hbm.at[:, :, :128], trial.at[0]), (trial_hbm.at[:, :, 128:], trial.at[1]),
        (features_hbm, features_in), (mask_hbm, mask_in), (update_hbm, w_update),
        (atom_hbm, w_atom), (pair_hbm, w_pair), (bias_hbm, bias), (block_hbm, w_block),
    )
    for i, (source, target) in enumerate(pairs):
        copy = pltpu.make_async_copy(source, target, load_sem.at[i])
        copy.start()
        loads.append(copy)

    feature_copies, vector_copies = {}, {}
    for i, side in enumerate(SIDES):
        mine = (1 - side[1]) * 3 + (1 - side[0])
        feature_copies[side] = pltpu.make_async_remote_copy(
            src_ref=patches.at[4], dst_ref=patches.at[mine], send_sem=send_f.at[i], recv_sem=recv_f.at[i],
            device_id=device(side), device_id_type=MESH,
        )
        width = 2 if side[0] * side[1] < 0 else 3
        from_r, to_r = span(side[0], 4, width)
        from_c, to_c = span(side[1], 8, width)
        shift = lambda s: slice(3 + s.start, 3 + s.stop)
        vector_copies[side] = pltpu.make_async_remote_copy(
            src_ref=x_hi.at[shift(from_r), shift(from_c)], dst_ref=x_hi.at[to_r, to_c],
            send_sem=send_x.at[i], recv_sem=recv_x.at[i], device_id=device(side), device_id_type=MESH,
        )

    def send_features(sides):
        for side in sides:
            feature_copies[side].start()

    def send_vectors(sides):
        for side in sides:
            vector_copies[side].start()

    def send(sides):
        send_features(sides)
        send_vectors(sides)

    def answer():
        pl.semaphore_wait(barrier, len(FORWARD))
        for side in FORWARD:
            pl.semaphore_signal(answered, inc=1, device_id=device(side), device_id_type=MESH)

    pl.when(last)(answer)

    loads[2].wait()
    patches[4, :, :128] = features_in[...].astype(F32).reshape(32, 128).astype(BF16)
    loads[3].wait()
    diagonal = (iota((4, 8, 8), 1) == iota((4, 8, 8), 2)).astype(F32)
    wide = jnp.zeros((4, 8, 128), F32)
    for k in range(3):
        by_row = jnp.broadcast_to(mask_in[k].astype(F32)[:, None, :], (4, 8, 8))
        in_mask = jnp.sum(by_row * diagonal, axis=2, keepdims=True)
        wide = wide + jnp.where(iota((4, 8, 128), 2) == k, in_mask, 0.0)
    patches[4, :, 128:] = wide.reshape(32, 128).astype(BF16)
    pl.when(last)(lambda: send_features(FORWARD))
    loads[0].wait()
    loads[1].wait()
    trial_pad = jnp.zeros((PAD - ORBITALS, 256), F32)

    def convert(columns):
        for r in range(4):
            for c in columns:
                atom = jnp.concatenate(
                    [trial[h, r, pl.ds(c, ORBITALS, stride=8), :] for h in range(2)], axis=1
                )
                atom = jnp.concatenate([atom, trial_pad], axis=0)
                high = atom.astype(BF16)
                x_hi[3 + r, 3 + c] = high
                x_lo[3 + r, 3 + c] = (atom - high.astype(F32)).astype(BF16)

    convert(range(5, 8))
    pl.when(last)(lambda: send_vectors(FORWARD))
    convert(range(5))

    def send_all():
        pl.semaphore_wait(barrier, jnp.where(first, 2, 8))
        send(ACROSS)
        pl.when(jnp.logical_not(first))(lambda: send(FORWARD + BACKWARD))

    pl.when(jnp.logical_not(last))(send_all)

    for rows, columns in ((0, slice(11, 14)), (slice(1, 3), 13), (9, slice(0, 3)), (slice(7, 9), 0)):
        x_hi[rows, columns] = jnp.zeros_like(x_hi[rows, columns])
    for rows, columns in (
        (slice(0, 3), slice(0, 14)), (slice(7, 10), slice(0, 14)), (slice(3, 7), slice(0, 3)), (slice(3, 7), slice(11, 14))
    ):
        x_lo[rows, columns] = jnp.zeros_like(x_lo[rows, columns])

    for i in range(4, 9):
        loads[i].wait()
    for i, (_, _, base, slot, transposed) in enumerate(BLOCKS):
        placed[i] = place_weights(w_block[...], base, transposed)
    placed[7] = place_weights(w_block[...], BLOCKS[3][2], True)
    y_hi[...] = jnp.zeros_like(y_hi)
    z_hi[...] = jnp.zeros_like(z_hi)
    h_full[...] = jnp.zeros_like(h_full)

    point = iota((160, 1), 0)
    cell = iota((1, 192), 1)
    patch = cell >> 5
    patch_column = (patch >= 3).astype(jnp.int32)
    cell_row = (patch - 3 * patch_column) * 4 - 4 + ((cell >> 3) & 3)
    for i, (first_patch, first_point) in enumerate(((0, 1), (-8, -3))):
        down = cell_row - ((point & 15) - 3)
        right = (patch_column * 8 + first_patch + (cell & 7)) - ((point >> 4) + first_point)
        same = (down == 0) & (right == 0)
        near = (jnp.abs(down) <= 1) & (jnp.abs(right) <= 1) & (down + right != 0) | (
            (down == right) & (jnp.abs(down) == 1)
        )
        select[i] = same.astype(F32).astype(BF16)
        gather[i] = near.astype(F32).astype(BF16)

    lane_slot = iota((8, 128), 1) >> 4

    def build(left):
        i, columns = (1, 6) if left else (0, 10)
        atoms, wide = columns * 16, columns - 2
        around = (patches[:6] if left else patches[3:]).reshape(192, 256)
        picked = jnp.dot(select[i, :atoms], around, preferred_element_type=F32)
        gathered = jnp.dot(gather[i, :atoms], around[:, :128], preferred_element_type=F32)
        own = picked[:, :128]
        update = jax.nn.silu(jnp.dot(gathered.astype(BF16), w_update[...], preferred_element_type=F32))
        refined = (own + update).astype(BF16)
        shape = (columns, 16, 128)
        self_part[:columns] = jnp.dot(refined, w_atom[...], preferred_element_type=F32).reshape(shape)
        pair_part[:columns] = jnp.dot(own.astype(BF16), w_pair[...], preferred_element_type=F32).reshape(shape)
        masks[:columns] = picked[:, 128:].reshape(shape)

        for i, (dr, dc, _, slot, transposed) in enumerate(BLOCKS):
            r0, c0 = (1 + dr, 1 + dc) if transposed else (1, 1)
            r1, c1 = (1, 1) if transposed else (1 + dr, 1 + dc)
            message = jax.nn.silu(
                self_part[c0 : c0 + wide, r0 : r0 + 8]
                + pair_part[c1 : c1 + wide, r1 : r1 + 8]
                + bias[slot : slot + 1]
            )
            if slot < 3:
                message = message * masks[c0 : c0 + wide, r0 : r0 + 8, slot : slot + 1]
            message = message.astype(BF16).reshape(wide * 8, 128)
            block = jnp.dot(message, placed[i], preferred_element_type=F32)
            if slot == 3:
                block = 0.5 * (block + jnp.dot(message, placed[7], preferred_element_type=F32))
            blocks[i, :wide] = block.reshape(wide, 8, 256)

        for g in (0,) if left else (1, 2):
            for c in range(4):
                at = c + 4 * max(g - 1, 0)
                for a in range(ORBITALS):
                    half = slice(128 * (a // 8), 128 * (a // 8) + 128)
                    for part in range(2):
                        value = jnp.zeros((8, 128), F32)
                        for i, (_, _, base, _, _) in enumerate(BLOCKS):
                            if (base + c) // 8 == part:
                                value = jnp.where(lane_slot == (base - a) % 8, blocks[i, at, :, half], value)
                        turn = (c + a) * 16 % 128
                        if turn:
                            value = pltpu.roll(value, turn, axis=1)
                        h_full[g, part, pl.ds(c * 16 + a, 8, stride=64), :] = value

            def halves(r, carry):
                rows = pl.ds(pl.multiple_of(r * 64, 64), 64)
                full = jnp.concatenate([h_full[g, 0, rows, :], h_full[g, 1, rows, :]], axis=1)
                high = full.astype(BF16)
                h[g, r, :64] = high
                h[g, r, 64:] = (full - high.astype(F32)).astype(BF16)
                return carry

            lax.fori_loop(0, 8, halves, 0, unroll=UNROLL)

    def apply(vectors, r, g, begin=0, end=4):
        c = 1 + 4 * g
        weights = jnp.concatenate(
            [
                vectors[r, c - 1 : c + 4].reshape(80, 256),
                vectors[r + 1, c - 1 : c + 5].reshape(96, 256),
                vectors[r + 2, c : c + 5].reshape(80, 256),
            ],
            axis=0,
        )
        rows = slice(16 * begin, 16 * end)
        parts = jnp.concatenate([h[g, r, :64][rows], h[g, r, 64:][rows]], axis=0)
        total = jnp.dot(parts, weights, preferred_element_type=F32)
        size = 16 * (end - begin)
        return (total[:size] + total[size:]).reshape(end - begin, PAD, 256)

    def start(r, c, n):
        return x_hi[r, c : c + n].astype(F32) + x_lo[r, c : c + n].astype(F32)

    def first_step(groups):
        def row(r, carry):
            for g in groups:
                c = 1 + 4 * g
                value = (apply(x_hi, r, g) - CENTRE * start(r + 1, c, 4)) * (1.0 / HALF_WIDTH)
                y[r + 1, c : c + 4] = value
                y_hi[r + 1, c : c + 4] = value.astype(BF16)
            return carry

        lax.fori_loop(0, 8, row, 0, unroll=UNROLL)

    def second_step(groups):
        def row(r, carry):
            for g in groups:
                c = 1 + 4 * g
                value = (apply(y_hi, r, g) - CENTRE * y[r + 1, c : c + 4]) * (2.0 / HALF_WIDTH)
                value = value - start(r + 1, c, 4)
                z[r + 1, c : c + 4] = value
                z_hi[r + 1, c : c + 4] = value.astype(BF16)
            return carry

        lax.fori_loop(1, 7, row, 0, unroll=UNROLL)

    def third_row(r, carry):
        for g, begin, end in ((0, 2, 4), (1, 0, 4), (2, 0, 2)):
            c, n = 1 + 4 * g + begin, end - begin
            value = (apply(z_hi, r, g, begin, end) - CENTRE * z[r + 1, c : c + n]) * (2.0 / HALF_WIDTH)
            value = value - y[r + 1, c : c + n]
            for half in range(2):
                for k in range(n):
                    out_ref[pl.ds((r - 2) * 208 + half * 8 + c - 3 + k, ORBITALS, stride=16), :] = value[
                        k, :ORBITALS, 128 * half : 128 * half + 128
                    ]
        return carry

    def late():
        def send_back():
            pl.semaphore_wait(answered, len(BACKWARD))
            send(BACKWARD)

        pl.when(first)(send_back)
        feature_copies[FORWARD[2]].wait_recv()
        pl.when(last)(lambda: send(ACROSS))
        for side in FORWARD[:2]:
            feature_copies[side].wait_recv()
        pl.when(last)(lambda: send(BACKWARD))

    pl.when(last)(late)
    for side in BACKWARD:
        feature_copies[side].wait_recv()
    pl.when(first)(lambda: send(FORWARD))
    for side in ACROSS:
        feature_copies[side].wait_recv()
    build(left=False)
    for side in BACKWARD + ACROSS:
        vector_copies[side].wait_recv()
    first_step((1, 2))
    second_step((2,))

    pl.when(jnp.logical_not(last))(late)
    build(left=True)
    for side in FORWARD:
        vector_copies[side].wait_recv()
    first_step((0,))
    second_step((0, 1))
    lax.fori_loop(2, 6, third_row, 0, unroll=UNROLL)

    for side in SIDES:
        feature_copies[side].wait_send()
        vector_copies[side].wait_send()


def per_device(features, pair_mask, w_update, w_atom, w_pair, slot_bias, w_block, trial):
    pair_mask = pair_mask.transpose(2, 0, 1)
    w_block = w_block.T
    rows, columns, _, width = trial.shape
    trial = trial.transpose(0, 2, 1, 3).reshape(rows, ORBITALS * columns, width)
    halves = (2, rows, ORBITALS * columns, 128)
    vectors = (10, 14, PAD, 256)
    sides = pltpu.SemaphoreType.DMA((len(SIDES),))
    filtered = pl.pallas_call(
        kernel,
        name="filter",
        out_shape=jax.ShapeDtypeStruct((rows * ORBITALS * 2 * columns, 128), F32),
        in_specs=[pl.BlockSpec(memory_space=pltpu.HBM)] * 8,
        out_specs=pl.BlockSpec(memory_space=pltpu.VMEM),
        scratch_shapes=[
            pltpu.VMEM(features.shape, BF16),
            pltpu.VMEM(pair_mask.shape, jnp.int32),
            pltpu.VMEM(w_update.shape, BF16),
            pltpu.VMEM(w_atom.shape, BF16),
            pltpu.VMEM(w_pair.shape, BF16),
            pltpu.VMEM(slot_bias.shape, F32),
            pltpu.VMEM(w_block.shape, BF16),
            pltpu.VMEM(halves, F32),
            pltpu.VMEM((9, 32, 256), BF16),
            pltpu.VMEM(vectors, BF16),
            pltpu.VMEM(vectors, BF16),
            pltpu.VMEM(vectors, BF16),
            pltpu.VMEM(vectors, BF16),
            pltpu.VMEM(vectors, F32),
            pltpu.VMEM(vectors, F32),
            pltpu.VMEM((8, 128, 256), BF16),
            pltpu.VMEM((2, 160, 192), BF16),
            pltpu.VMEM((2, 160, 192), BF16),
            pltpu.VMEM((10, 16, 128), F32),
            pltpu.VMEM((10, 16, 128), F32),
            pltpu.VMEM((10, 16, 128), F32),
            pltpu.VMEM((7, 8, 8, 256), F32),
            pltpu.VMEM((3, 2, 512, 128), F32),
            pltpu.VMEM((3, 8, 128, 256), BF16),
            pltpu.SemaphoreType.DMA((9,)),
            pltpu.SemaphoreType.REGULAR,
            sides,
            sides,
            sides,
            sides,
        ],
        compiler_params=pltpu.CompilerParams(
            collective_id=0, has_side_effects=True, vmem_limit_bytes=40 * 2**20
        ),
    )(
        *(
            pltpu.with_memory_space_constraint(array, pltpu.HBM)
            for array in (features, pair_mask, w_update, w_atom, w_pair, slot_bias, w_block, trial)
        )
    )
    filtered = filtered.reshape(rows, ORBITALS, 2, columns, 128).transpose(0, 1, 3, 2, 4)
    return filtered.reshape(rows, ORBITALS, columns, width).transpose(0, 2, 1, 3)


def solution(mesh):
    return jax.shard_map(
        per_device,
        mesh=mesh,
        in_specs=(
            P("px", "py", None),
            P("px", "py", None),
            P(),
            P(),
            P(),
            P(),
            P(),
            P("px", "py", None, None),
        ),
        out_specs=P("px", "py", None, None),
        check_vma=False,
    )
```

```python
import functools

import jax
import jax.numpy as jnp
from jax import lax
from jax.experimental import pallas as pl
from jax.experimental.pallas import tpu as pltpu
from jax.sharding import PartitionSpec as P

ORBITALS = 13
PAD = 16
CENTRE = 4.0
HALF_WIDTH = 24.0
MESH = pl.DeviceIdType.MESH
F32 = jnp.float32
BF16 = jnp.bfloat16

FORWARD = ((1, 1), (-1, 1), (0, 1))
BACKWARD = ((-1, -1), (1, -1), (0, -1))
ACROSS = ((1, 0), (-1, 0))
SIDES = FORWARD + BACKWARD + ACROSS
LAYERS = 12
UNROLL = True
BLOCKS = (
    (-1, -1, 0, 2, True),
    (-1, 0, 1, 1, True),
    (0, -1, 5, 0, True),
    (0, 0, 6, 3, False),
    (0, 1, 7, 0, False),
    (1, 0, 11, 1, False),
    (1, 1, 12, 2, False),
)


def span(step, size, width):
    if step > 0:
        return slice(size - width, size), slice(3 - width, 3)
    if step < 0:
        return slice(0, width), slice(3 + size, 3 + size + width)
    return slice(0, size), slice(3, 3 + size)


def iota(shape, axis):
    return lax.broadcasted_iota(jnp.int32, shape, axis)


def place_weights(w_block, base, transposed):
    lane = iota((ORBITALS * ORBITALS, 256), 1)
    source = iota((ORBITALS * ORBITALS, 256), 0)
    b = lane & 15
    a = 8 * (lane >> 7) + ((base - ((lane >> 4) & 7)) & 7)
    entry = b * ORBITALS + a if transposed else a * ORBITALS + b
    chosen = (source == entry) & (a < ORBITALS) & (b < ORBITALS)
    return lax.dot_general(
        w_block, chosen.astype(F32).astype(BF16), (((0,), (0,)), ((), ())), preferred_element_type=F32
    ).astype(BF16)


def kernel(
    features_hbm, mask_hbm, update_hbm, atom_hbm, pair_hbm, bias_hbm, block_hbm, trial_hbm,
    out_ref,
    features_in, mask_in, w_update, w_atom, w_pair, bias, w_block, trial,
    patches, x_hi, x_lo, y_hi, z_hi, y, z, placed, gather, select,
    self_part, pair_part, masks, blocks, h_full, h,
    load_sem, answered, send_f, recv_f, send_x, recv_x,
):
    px, py = lax.axis_index("px"), lax.axis_index("py")
    nx, ny = lax.axis_size("px"), lax.axis_size("py")

    def device(side):
        return (lax.rem(px + side[0] + nx, nx), lax.rem(py + side[1] + ny, ny))

    layer = lax.rem(py, LAYERS)
    first, last = layer == 0, layer == LAYERS - 1

    def greet(sides):
        for side in sides:
            pl.semaphore_signal(barrier, inc=1, device_id=device(side), device_id_type=MESH)

    barrier = pltpu.get_barrier_semaphore()
    pl.when(layer != 1)(lambda: greet(BACKWARD))
    pl.when(jnp.logical_not(last))(lambda: greet(ACROSS))
    pl.when(layer < LAYERS - 2)(lambda: greet(FORWARD))

    loads = []
    pairs = (
        (trial_hbm.at[:, :, :128], trial.at[0]), (trial_hbm.at[:, :, 128:], trial.at[1]),
        (features_hbm, features_in), (mask_hbm, mask_in), (update_hbm, w_update),
        (atom_hbm, w_atom), (pair_hbm, w_pair), (bias_hbm, bias), (block_hbm, w_block),
    )
    for i, (source, target) in enumerate(pairs):
        copy = pltpu.make_async_copy(source, target, load_sem.at[i])
        copy.start()
        loads.append(copy)

    feature_copies, vector_copies = {}, {}
    for i, side in enumerate(SIDES):
        mine = (1 - side[1]) * 3 + (1 - side[0])
        near_columns = slice(16, 32) if side in FORWARD else slice(0, 16) if side in BACKWARD else slice(0, 32)
        feature_copies[side] = pltpu.make_async_remote_copy(
            src_ref=patches.at[4, near_columns], dst_ref=patches.at[mine, near_columns], send_sem=send_f.at[i], recv_sem=recv_f.at[i],
            device_id=device(side), device_id_type=MESH,
        )
        width = 2 if side[0] * side[1] < 0 else 3
        from_r, to_r = span(side[0], 4, width)
        from_c, to_c = span(side[1], 8, width)
        shift = lambda s: slice(3 + s.start, 3 + s.stop)
        vector_copies[side] = pltpu.make_async_remote_copy(
            src_ref=x_hi.at[shift(from_r), shift(from_c)], dst_ref=x_hi.at[to_r, to_c],
            send_sem=send_x.at[i], recv_sem=recv_x.at[i], device_id=device(side), device_id_type=MESH,
        )

    def send_features(sides):
        for side in sides:
            feature_copies[side].start()

    def send_vectors(sides):
        for side in sides:
            vector_copies[side].start()

    def send(sides):
        send_features(sides)
        send_vectors(sides)

    def answer():
        pl.semaphore_wait(barrier, len(FORWARD))
        for side in FORWARD:
            pl.semaphore_signal(answered, inc=1, device_id=device(side), device_id_type=MESH)

    pl.when(last)(answer)

    loads[2].wait()
    atoms = features_in[...].astype(F32).reshape(32, 128)
    loads[3].wait()
    diagonal = (iota((4, 8, 8), 1) == iota((4, 8, 8), 2)).astype(F32)
    wide = jnp.zeros((4, 8, 128), F32)
    for k in range(3):
        by_row = jnp.broadcast_to(mask_in[k].astype(F32)[:, None, :], (4, 8, 8))
        in_mask = jnp.sum(by_row * diagonal, axis=2, keepdims=True)
        wide = wide + jnp.where(iota((4, 8, 128), 2) == k, in_mask, 0.0)
    atoms = jnp.concatenate([atoms, wide.reshape(32, 128)], axis=1).astype(BF16)
    by_column = (iota((32, 32), 0) >> 2) + 8 * (iota((32, 32), 0) & 3) == iota((32, 32), 1)
    patches[4] = jnp.dot(by_column.astype(F32).astype(BF16), atoms, preferred_element_type=F32).astype(BF16)
    pl.when(last)(lambda: send_features(FORWARD))
    loads[0].wait()
    loads[1].wait()
    trial_pad = jnp.zeros((PAD - ORBITALS, 256), F32)

    def convert(columns):
        for r in range(4):
            for c in columns:
                atom = jnp.concatenate(
                    [trial[h, r, pl.ds(c, ORBITALS, stride=8), :] for h in range(2)], axis=1
                )
                atom = jnp.concatenate([atom, trial_pad], axis=0)
                high = atom.astype(BF16)
                x_hi[3 + r, 3 + c] = high
                x_lo[3 + r, 3 + c] = (atom - high.astype(F32)).astype(BF16)

    convert(range(5, 8))
    pl.when(last)(lambda: send_vectors(FORWARD))
    convert(range(5))

    def send_all():
        pl.semaphore_wait(barrier, jnp.where(first, 2, 8))
        send(ACROSS)
        pl.when(jnp.logical_not(first))(lambda: send(FORWARD + BACKWARD))

    pl.when(jnp.logical_not(last))(send_all)

    patches[:3, :16] = jnp.zeros((3, 16, 256), BF16)
    patches[6:, 16:] = jnp.zeros((3, 16, 256), BF16)
    for rows, columns in ((0, slice(11, 14)), (slice(1, 3), 13), (9, slice(0, 3)), (slice(7, 9), 0)):
        x_hi[rows, columns] = jnp.zeros_like(x_hi[rows, columns])
    for rows, columns in (
        (slice(0, 3), slice(0, 14)), (slice(7, 10), slice(0, 14)), (slice(3, 7), slice(0, 3)), (slice(3, 7), slice(11, 14))
    ):
        x_lo[rows, columns] = jnp.zeros_like(x_lo[rows, columns])

    for i in range(4, 9):
        loads[i].wait()
    for i, (_, _, base, slot, transposed) in enumerate(BLOCKS):
        placed[i] = place_weights(w_block[...], base, transposed)
    placed[7] = place_weights(w_block[...], BLOCKS[3][2], True)
    y_hi[...] = jnp.zeros_like(y_hi)
    z_hi[...] = jnp.zeros_like(z_hi)
    h_full[...] = jnp.zeros_like(h_full)

    point = iota((160, 1), 0)
    cell = iota((1, 192), 1)
    patch = cell >> 5
    patch_column = (patch >= 3).astype(jnp.int32)
    cell_row = (patch - 3 * patch_column) * 4 - 4 + (cell & 3)
    for i, (first_patch, first_point) in enumerate(((0, 1), (-8, -3))):
        down = cell_row - ((point & 15) - 3)
        right = (patch_column * 8 + first_patch + ((cell >> 2) & 7)) - ((point >> 4) + first_point)
        same = (down == 0) & (right == 0)
        near = (jnp.abs(down) <= 1) & (jnp.abs(right) <= 1) & (down + right != 0) | (
            (down == right) & (jnp.abs(down) == 1)
        )
        select[i] = same.astype(F32).astype(BF16)
        gather[i] = near.astype(F32).astype(BF16)

    lane_slot = iota((8, 128), 1) >> 4

    def build(left):
        i, columns = (1, 6) if left else (0, 10)
        atoms, wide = columns * 16, columns - 2
        around = (patches[:6] if left else patches[3:]).reshape(192, 256)
        picked = jnp.dot(select[i, :atoms], around, preferred_element_type=F32)
        gathered = jnp.dot(gather[i, :atoms], around[:, :128], preferred_element_type=F32)
        own = picked[:, :128]
        update = jax.nn.silu(jnp.dot(gathered.astype(BF16), w_update[...], preferred_element_type=F32))
        refined = (own + update).astype(BF16)
        shape = (columns, 16, 128)
        self_part[:columns] = jnp.dot(refined, w_atom[...], preferred_element_type=F32).reshape(shape)
        pair_part[:columns] = jnp.dot(own.astype(BF16), w_pair[...], preferred_element_type=F32).reshape(shape)
        masks[:columns] = picked[:, 128:].reshape(shape)

        for i, (dr, dc, _, slot, transposed) in enumerate(BLOCKS):
            r0, c0 = (1 + dr, 1 + dc) if transposed else (1, 1)
            r1, c1 = (1, 1) if transposed else (1 + dr, 1 + dc)
            message = jax.nn.silu(
                self_part[c0 : c0 + wide, r0 : r0 + 8]
                + pair_part[c1 : c1 + wide, r1 : r1 + 8]
                + bias[slot : slot + 1]
            )
            if slot < 3:
                message = message * masks[c0 : c0 + wide, r0 : r0 + 8, slot : slot + 1]
            message = message.astype(BF16).reshape(wide * 8, 128)
            block = jnp.dot(message, placed[i], preferred_element_type=F32)
            if slot == 3:
                block = 0.5 * (block + jnp.dot(message, placed[7], preferred_element_type=F32))
            blocks[i, :wide] = block.reshape(wide, 8, 256)

        for g in (0,) if left else (1, 2):
            for c in range(4):
                at = c + 4 * max(g - 1, 0)
                for a in range(ORBITALS):
                    half = slice(128 * (a // 8), 128 * (a // 8) + 128)
                    for part in range(2):
                        value = jnp.zeros((8, 128), F32)
                        for i, (_, _, base, _, _) in enumerate(BLOCKS):
                            if (base + c) // 8 == part:
                                value = jnp.where(lane_slot == (base - a) % 8, blocks[i, at, :, half], value)
                        turn = (c + a) * 16 % 128
                        if turn:
                            value = pltpu.roll(value, turn, axis=1)
                        h_full[g, part, pl.ds(c * 16 + a, 8, stride=64), :] = value

            def halves(r, carry):
                rows = pl.ds(pl.multiple_of(r * 64, 64), 64)
                full = jnp.concatenate([h_full[g, 0, rows, :], h_full[g, 1, rows, :]], axis=1)
                high = full.astype(BF16)
                h[g, r, :64] = high
                h[g, r, 64:] = (full - high.astype(F32)).astype(BF16)
                return carry

            lax.fori_loop(0, 8, halves, 0, unroll=UNROLL)

    def apply(vectors, r, g, begin=0, end=4):
        c = 1 + 4 * g
        weights = jnp.concatenate(
            [
                vectors[r, c - 1 : c + 4].reshape(80, 256),
                vectors[r + 1, c - 1 : c + 5].reshape(96, 256),
                vectors[r + 2, c : c + 5].reshape(80, 256),
            ],
            axis=0,
        )
        rows = slice(16 * begin, 16 * end)
        parts = jnp.concatenate([h[g, r, :64][rows], h[g, r, 64:][rows]], axis=0)
        total = jnp.dot(parts, weights, preferred_element_type=F32)
        size = 16 * (end - begin)
        return (total[:size] + total[size:]).reshape(end - begin, PAD, 256)

    def start(r, c, n):
        return x_hi[r, c : c + n].astype(F32) + x_lo[r, c : c + n].astype(F32)

    def first_step(groups):
        def row(r, carry):
            for g in groups:
                c = 1 + 4 * g
                value = (apply(x_hi, r, g) - CENTRE * start(r + 1, c, 4)) * (1.0 / HALF_WIDTH)
                y[r + 1, c : c + 4] = value
                y_hi[r + 1, c : c + 4] = value.astype(BF16)
            return carry

        lax.fori_loop(0, 8, row, 0, unroll=UNROLL)

    def second_step(groups):
        def row(r, carry):
            for g in groups:
                c = 1 + 4 * g
                value = (apply(y_hi, r, g) - CENTRE * y[r + 1, c : c + 4]) * (2.0 / HALF_WIDTH)
                value = value - start(r + 1, c, 4)
                z[r + 1, c : c + 4] = value
                z_hi[r + 1, c : c + 4] = value.astype(BF16)
            return carry

        lax.fori_loop(1, 7, row, 0, unroll=UNROLL)

    def third_row(r, carry):
        for g, begin, end in ((0, 2, 4), (1, 0, 4), (2, 0, 2)):
            c, n = 1 + 4 * g + begin, end - begin
            value = (apply(z_hi, r, g, begin, end) - CENTRE * z[r + 1, c : c + n]) * (2.0 / HALF_WIDTH)
            value = value - y[r + 1, c : c + n]
            for half in range(2):
                for k in range(n):
                    out_ref[pl.ds((r - 2) * 208 + half * 8 + c - 3 + k, ORBITALS, stride=16), :] = value[
                        k, :ORBITALS, 128 * half : 128 * half + 128
                    ]
        return carry

    def late():
        def send_back():
            pl.semaphore_wait(answered, len(BACKWARD))
            send(BACKWARD)

        pl.when(first)(send_back)
        feature_copies[FORWARD[2]].wait_recv()
        pl.when(last)(lambda: send(ACROSS))
        for side in FORWARD[:2]:
            feature_copies[side].wait_recv()
        pl.when(last)(lambda: send(BACKWARD))

    pl.when(last)(late)
    for side in BACKWARD:
        feature_copies[side].wait_recv()
    pl.when(first)(lambda: send(FORWARD))
    for side in ACROSS:
        feature_copies[side].wait_recv()
    build(left=False)

    @pl.when(jnp.logical_not(first))
    def _():
        pl.when(jnp.logical_not(last))(late)
        build(left=True)

    for side in BACKWARD + ACROSS:
        vector_copies[side].wait_recv()
    first_step((1, 2))
    second_step((2,))

    @pl.when(first)
    def _():
        late()
        build(left=True)

    for side in FORWARD:
        vector_copies[side].wait_recv()
    first_step((0,))
    second_step((0, 1))
    lax.fori_loop(2, 6, third_row, 0, unroll=UNROLL)

    for side in SIDES:
        feature_copies[side].wait_send()
        vector_copies[side].wait_send()


def per_device(features, pair_mask, w_update, w_atom, w_pair, slot_bias, w_block, trial):
    pair_mask = pair_mask.transpose(2, 0, 1)
    w_block = w_block.T
    rows, columns, _, width = trial.shape
    trial = trial.transpose(0, 2, 1, 3).reshape(rows, ORBITALS * columns, width)
    halves = (2, rows, ORBITALS * columns, 128)
    vectors = (10, 14, PAD, 256)
    sides = pltpu.SemaphoreType.DMA((len(SIDES),))
    filtered = pl.pallas_call(
        kernel,
        name="filter",
        out_shape=jax.ShapeDtypeStruct((rows * ORBITALS * 2 * columns, 128), F32),
        in_specs=[pl.BlockSpec(memory_space=pltpu.HBM)] * 8,
        out_specs=pl.BlockSpec(memory_space=pltpu.VMEM),
        scratch_shapes=[
            pltpu.VMEM(features.shape, BF16),
            pltpu.VMEM(pair_mask.shape, jnp.int32),
            pltpu.VMEM(w_update.shape, BF16),
            pltpu.VMEM(w_atom.shape, BF16),
            pltpu.VMEM(w_pair.shape, BF16),
            pltpu.VMEM(slot_bias.shape, F32),
            pltpu.VMEM(w_block.shape, BF16),
            pltpu.VMEM(halves, F32),
            pltpu.VMEM((9, 32, 256), BF16),
            pltpu.VMEM(vectors, BF16),
            pltpu.VMEM(vectors, BF16),
            pltpu.VMEM(vectors, BF16),
            pltpu.VMEM(vectors, BF16),
            pltpu.VMEM(vectors, F32),
            pltpu.VMEM(vectors, F32),
            pltpu.VMEM((8, 128, 256), BF16),
            pltpu.VMEM((2, 160, 192), BF16),
            pltpu.VMEM((2, 160, 192), BF16),
            pltpu.VMEM((10, 16, 128), F32),
            pltpu.VMEM((10, 16, 128), F32),
            pltpu.VMEM((10, 16, 128), F32),
            pltpu.VMEM((7, 8, 8, 256), F32),
            pltpu.VMEM((3, 2, 512, 128), F32),
            pltpu.VMEM((3, 8, 128, 256), BF16),
            pltpu.SemaphoreType.DMA((9,)),
            pltpu.SemaphoreType.REGULAR,
            sides,
            sides,
            sides,
            sides,
        ],
        compiler_params=pltpu.CompilerParams(
            collective_id=0, has_side_effects=True, vmem_limit_bytes=40 * 2**20
        ),
    )(
        *(
            pltpu.with_memory_space_constraint(array, pltpu.HBM)
            for array in (features, pair_mask, w_update, w_atom, w_pair, slot_bias, w_block, trial)
        )
    )
    filtered = filtered.reshape(rows, ORBITALS, 2, columns, 128).transpose(0, 1, 3, 2, 4)
    return filtered.reshape(rows, ORBITALS, columns, width).transpose(0, 2, 1, 3)


def solution(mesh):
    return jax.shard_map(
        per_device,
        mesh=mesh,
        in_specs=(
            P("px", "py", None),
            P("px", "py", None),
            P(),
            P(),
            P(),
            P(),
            P(),
            P("px", "py", None, None),
        ),
        out_specs=P("px", "py", None, None),
        check_vma=False,
    )
```

```python
import functools

import jax
import jax.numpy as jnp
from jax import lax
from jax.experimental import pallas as pl
from jax.experimental.pallas import tpu as pltpu
from jax.sharding import PartitionSpec as P

ORBITALS = 13
PAD = 16
CENTRE = 4.0
HALF_WIDTH = 24.0
MESH = pl.DeviceIdType.MESH
F32 = jnp.float32
BF16 = jnp.bfloat16

FORWARD = ((1, 1), (-1, 1), (0, 1))
BACKWARD = ((-1, -1), (1, -1), (0, -1))
ACROSS = ((1, 0), (-1, 0))
SIDES = FORWARD + BACKWARD + ACROSS
LAYERS = 12
UNROLL = True
BLOCKS = (
    (-1, -1, 0, 2, True),
    (-1, 0, 1, 1, True),
    (0, -1, 5, 0, True),
    (0, 0, 6, 3, False),
    (0, 1, 7, 0, False),
    (1, 0, 11, 1, False),
    (1, 1, 12, 2, False),
)


def span(step, size, width):
    if step > 0:
        return slice(size - width, size), slice(3 - width, 3)
    if step < 0:
        return slice(0, width), slice(3 + size, 3 + size + width)
    return slice(0, size), slice(3, 3 + size)


def iota(shape, axis):
    return lax.broadcasted_iota(jnp.int32, shape, axis)


def place_weights(w_block, base, transposed):
    lane = iota((ORBITALS * ORBITALS, 256), 1)
    source = iota((ORBITALS * ORBITALS, 256), 0)
    b = lane & 15
    a = 8 * (lane >> 7) + ((base - ((lane >> 4) & 7)) & 7)
    entry = b * ORBITALS + a if transposed else a * ORBITALS + b
    chosen = (source == entry) & (a < ORBITALS) & (b < ORBITALS)
    return lax.dot_general(
        w_block, chosen.astype(F32).astype(BF16), (((0,), (0,)), ((), ())), preferred_element_type=F32
    ).astype(BF16)


def kernel(
    features_hbm, mask_hbm, update_hbm, atom_hbm, pair_hbm, bias_hbm, block_hbm, trial_hbm,
    out_ref,
    features_in, mask_in, w_update, w_atom, w_pair, bias, w_block, trial,
    patches, x_hi, x_lo, y_hi, z_hi, y, z, placed, gather, select,
    self_part, pair_part, masks, blocks, h_full, h,
    load_sem, answered, send_f, recv_f, send_x, recv_x,
):
    px, py = lax.axis_index("px"), lax.axis_index("py")
    nx, ny = lax.axis_size("px"), lax.axis_size("py")

    def device(side):
        return (lax.rem(px + side[0] + nx, nx), lax.rem(py + side[1] + ny, ny))

    layer = lax.rem(py, LAYERS)
    first, last = layer == 0, layer == LAYERS - 1

    def greet(sides):
        for side in sides:
            pl.semaphore_signal(barrier, inc=1, device_id=device(side), device_id_type=MESH)

    barrier = pltpu.get_barrier_semaphore()
    pl.when(layer != 1)(lambda: greet(BACKWARD))
    pl.when(jnp.logical_not(last))(lambda: greet(ACROSS))
    pl.when(layer < LAYERS - 2)(lambda: greet(FORWARD))

    loads = []
    pairs = (
        (trial_hbm.at[:, :, :128], trial.at[0]), (trial_hbm.at[:, :, 128:], trial.at[1]),
        (features_hbm, features_in), (mask_hbm, mask_in), (update_hbm, w_update),
        (atom_hbm, w_atom), (pair_hbm, w_pair), (bias_hbm, bias), (block_hbm, w_block),
    )
    for i, (source, target) in enumerate(pairs):
        copy = pltpu.make_async_copy(source, target, load_sem.at[i])
        copy.start()
        loads.append(copy)

    feature_copies, vector_copies = {}, {}
    for i, side in enumerate(SIDES):
        mine = (1 - side[1]) * 3 + (1 - side[0])
        near_columns = slice(16, 32) if side in FORWARD else slice(0, 16) if side in BACKWARD else slice(0, 32)
        feature_copies[side] = pltpu.make_async_remote_copy(
            src_ref=patches.at[4, near_columns], dst_ref=patches.at[mine, near_columns], send_sem=send_f.at[i], recv_sem=recv_f.at[i],
            device_id=device(side), device_id_type=MESH,
        )
        width = 2 if side[0] * side[1] < 0 else 3
        from_r, to_r = span(side[0], 4, width)
        from_c, to_c = span(side[1], 8, width)
        shift = lambda s: slice(3 + s.start, 3 + s.stop)
        vector_copies[side] = pltpu.make_async_remote_copy(
            src_ref=x_hi.at[shift(from_r), shift(from_c)], dst_ref=x_hi.at[to_r, to_c],
            send_sem=send_x.at[i], recv_sem=recv_x.at[i], device_id=device(side), device_id_type=MESH,
        )

    def send_features(sides):
        for side in sides:
            feature_copies[side].start()

    def send_vectors(sides):
        for side in sides:
            vector_copies[side].start()

    def send(sides):
        send_features(sides)
        send_vectors(sides)

    def answer():
        pl.semaphore_wait(barrier, len(FORWARD))
        for side in FORWARD:
            pl.semaphore_signal(answered, inc=1, device_id=device(side), device_id_type=MESH)

    pl.when(last)(answer)

    loads[2].wait()
    atoms = features_in[...].astype(F32).reshape(32, 128)
    loads[3].wait()
    diagonal = (iota((4, 8, 8), 1) == iota((4, 8, 8), 2)).astype(F32)
    wide = jnp.zeros((4, 8, 128), F32)
    for k in range(3):
        by_row = jnp.broadcast_to(mask_in[k].astype(F32)[:, None, :], (4, 8, 8))
        in_mask = jnp.sum(by_row * diagonal, axis=2, keepdims=True)
        wide = wide + jnp.where(iota((4, 8, 128), 2) == k, in_mask, 0.0)
    atoms = jnp.concatenate([atoms, wide.reshape(32, 128)], axis=1).astype(BF16)
    by_column = (iota((32, 32), 0) >> 2) + 8 * (iota((32, 32), 0) & 3) == iota((32, 32), 1)
    patches[4] = jnp.dot(by_column.astype(F32).astype(BF16), atoms, preferred_element_type=F32).astype(BF16)
    pl.when(last)(lambda: send_features(FORWARD))
    loads[0].wait()
    loads[1].wait()
    trial_pad = jnp.zeros((PAD - ORBITALS, 256), F32)

    def convert(columns):
        for r in range(4):
            for c in columns:
                atom = jnp.concatenate(
                    [trial[h, r, pl.ds(c, ORBITALS, stride=8), :] for h in range(2)], axis=1
                )
                atom = jnp.concatenate([atom, trial_pad], axis=0)
                high = atom.astype(BF16)
                x_hi[3 + r, 3 + c] = high
                x_lo[3 + r, 3 + c] = (atom - high.astype(F32)).astype(BF16)

    convert(range(5, 8))
    pl.when(last)(lambda: send_vectors(FORWARD))
    convert(range(5))

    def send_all():
        pl.semaphore_wait(barrier, jnp.where(first, 2, 8))
        send(ACROSS)
        pl.when(jnp.logical_not(first))(lambda: send(FORWARD + BACKWARD))

    pl.when(jnp.logical_not(last))(send_all)

    patches[:3, :16] = jnp.zeros((3, 16, 256), BF16)
    patches[6:, 16:] = jnp.zeros((3, 16, 256), BF16)
    for rows, columns in ((0, slice(11, 14)), (slice(1, 3), 13), (9, slice(0, 3)), (slice(7, 9), 0)):
        x_hi[rows, columns] = jnp.zeros_like(x_hi[rows, columns])
    for rows, columns in (
        (slice(0, 3), slice(0, 14)), (slice(7, 10), slice(0, 14)), (slice(3, 7), slice(0, 3)), (slice(3, 7), slice(11, 14))
    ):
        x_lo[rows, columns] = jnp.zeros_like(x_lo[rows, columns])

    for i in range(4, 9):
        loads[i].wait()
    for i, (_, _, base, slot, transposed) in enumerate(BLOCKS):
        placed[i] = place_weights(w_block[...], base, transposed)
    placed[7] = place_weights(w_block[...], BLOCKS[3][2], True)
    y_hi[...] = jnp.zeros_like(y_hi)
    z_hi[...] = jnp.zeros_like(z_hi)
    h_full[...] = jnp.zeros_like(h_full)

    point = iota((160, 1), 0)
    cell = iota((1, 192), 1)
    patch = cell >> 5
    patch_column = (patch >= 3).astype(jnp.int32)
    cell_row = (patch - 3 * patch_column) * 4 - 4 + (cell & 3)
    for i, (first_patch, first_point) in enumerate(((0, 1), (-8, -3))):
        down = cell_row - ((point & 15) - 3)
        right = (patch_column * 8 + first_patch + ((cell >> 2) & 7)) - ((point >> 4) + first_point)
        same = (down == 0) & (right == 0)
        near = (jnp.abs(down) <= 1) & (jnp.abs(right) <= 1) & (down + right != 0) | (
            (down == right) & (jnp.abs(down) == 1)
        )
        select[i] = same.astype(F32).astype(BF16)
        gather[i] = near.astype(F32).astype(BF16)

    lane_slot = iota((8, 128), 1) >> 4

    def build(left):
        i, columns = (1, 6) if left else (0, 10)
        atoms, wide = columns * 16, columns - 2
        around = (patches[:6] if left else patches[3:]).reshape(192, 256)
        picked = jnp.dot(select[i, :atoms], around, preferred_element_type=F32)
        gathered = jnp.dot(gather[i, :atoms], around[:, :128], preferred_element_type=F32)
        own = picked[:, :128]
        update = jax.nn.silu(jnp.dot(gathered.astype(BF16), w_update[...], preferred_element_type=F32))
        refined = (own + update).astype(BF16)
        shape = (columns, 16, 128)
        self_part[:columns] = jnp.dot(refined, w_atom[...], preferred_element_type=F32).reshape(shape)
        pair_part[:columns] = jnp.dot(own.astype(BF16), w_pair[...], preferred_element_type=F32).reshape(shape)
        masks[:columns] = picked[:, 128:].reshape(shape)

        for i, (dr, dc, _, slot, transposed) in enumerate(BLOCKS):
            r0, c0 = (1 + dr, 1 + dc) if transposed else (1, 1)
            r1, c1 = (1, 1) if transposed else (1 + dr, 1 + dc)
            message = jax.nn.silu(
                self_part[c0 : c0 + wide, r0 : r0 + 8]
                + pair_part[c1 : c1 + wide, r1 : r1 + 8]
                + bias[slot : slot + 1]
            )
            if slot < 3:
                message = message * masks[c0 : c0 + wide, r0 : r0 + 8, slot : slot + 1]
            message = message.astype(BF16).reshape(wide * 8, 128)
            block = jnp.dot(message, placed[i], preferred_element_type=F32)
            if slot == 3:
                block = 0.5 * (block + jnp.dot(message, placed[7], preferred_element_type=F32))
            blocks[i, :wide] = block.reshape(wide, 8, 256)

        for g in (0,) if left else (1, 2):
            for c in range(4):
                at = c + 4 * max(g - 1, 0)
                for a in range(ORBITALS):
                    half = slice(128 * (a // 8), 128 * (a // 8) + 128)
                    for part in range(2):
                        value = jnp.zeros((8, 128), F32)
                        for i, (_, _, base, _, _) in enumerate(BLOCKS):
                            if (base + c) // 8 == part:
                                value = jnp.where(lane_slot == (base - a) % 8, blocks[i, at, :, half], value)
                        turn = (c + a) * 16 % 128
                        if turn:
                            value = pltpu.roll(value, turn, axis=1)
                        h_full[g, part, pl.ds(c * 16 + a, 8, stride=64), :] = value

            def halves(r, carry):
                rows = pl.ds(pl.multiple_of(r * 64, 64), 64)
                full = jnp.concatenate([h_full[g, 0, rows, :], h_full[g, 1, rows, :]], axis=1)
                high = full.astype(BF16)
                h[g, r, :64] = high
                h[g, r, 64:] = (full - high.astype(F32)).astype(BF16)
                return carry

            lax.fori_loop(0, 8, halves, 0, unroll=UNROLL)

    def apply(vectors, r, g, begin=0, end=4):
        c = 1 + 4 * g
        weights = jnp.concatenate(
            [
                vectors[r, c - 1 : c + 4].reshape(80, 256),
                vectors[r + 1, c - 1 : c + 5].reshape(96, 256),
                vectors[r + 2, c : c + 5].reshape(80, 256),
            ],
            axis=0,
        )
        rows = slice(16 * begin, 16 * end)
        parts = jnp.concatenate([h[g, r, :64][rows], h[g, r, 64:][rows]], axis=0)
        total = jnp.dot(parts, weights, preferred_element_type=F32)
        size = 16 * (end - begin)
        return (total[:size] + total[size:]).reshape(end - begin, PAD, 256)

    def start(r, c, n):
        return x_hi[r, c : c + n].astype(F32) + x_lo[r, c : c + n].astype(F32)

    def first_step(groups):
        def row(r, carry):
            for g in groups:
                c = 1 + 4 * g
                value = (apply(x_hi, r, g) - CENTRE * start(r + 1, c, 4)) * (1.0 / HALF_WIDTH)
                y[r + 1, c : c + 4] = value
                y_hi[r + 1, c : c + 4] = value.astype(BF16)
            return carry

        lax.fori_loop(0, 8, row, 0, unroll=UNROLL)

    def second_step(parts):
        def row(r, carry):
            for g, begin, end in parts:
                c, n = 1 + 4 * g + begin, end - begin
                value = (apply(y_hi, r, g, begin, end) - CENTRE * y[r + 1, c : c + n]) * (2.0 / HALF_WIDTH)
                value = value - start(r + 1, c, n)
                z[r + 1, c : c + n] = value
                z_hi[r + 1, c : c + n] = value.astype(BF16)
            return carry

        lax.fori_loop(1, 7, row, 0, unroll=UNROLL)

    def third_row(parts, r, carry):
        for g, begin, end in parts:
            c, n = 1 + 4 * g + begin, end - begin
            value = (apply(z_hi, r, g, begin, end) - CENTRE * z[r + 1, c : c + n]) * (2.0 / HALF_WIDTH)
            value = value - y[r + 1, c : c + n]
            for half in range(2):
                for k in range(n):
                    out_ref[pl.ds((r - 2) * 208 + half * 8 + c - 3 + k, ORBITALS, stride=16), :] = value[
                        k, :ORBITALS, 128 * half : 128 * half + 128
                    ]
        return carry

    def third_step(parts):
        lax.fori_loop(2, 6, functools.partial(third_row, parts), 0, unroll=UNROLL)

    def late():
        def send_back():
            pl.semaphore_wait(answered, len(BACKWARD))
            send(BACKWARD)

        pl.when(first)(send_back)
        feature_copies[FORWARD[2]].wait_recv()
        pl.when(last)(lambda: send(ACROSS))
        for side in FORWARD[:2]:
            feature_copies[side].wait_recv()
        pl.when(last)(lambda: send(BACKWARD))

    pl.when(last)(late)
    for side in BACKWARD:
        feature_copies[side].wait_recv()
    pl.when(first)(lambda: send(FORWARD))
    for side in ACROSS:
        feature_copies[side].wait_recv()
    build(left=False)

    @pl.when(jnp.logical_not(first))
    def _():
        pl.when(jnp.logical_not(last))(late)
        build(left=True)

    for side in BACKWARD + ACROSS:
        vector_copies[side].wait_recv()
    first_step((1, 2))
    second_step(((1, 1, 4), (2, 0, 3)))
    third_step(((1, 2, 4), (2, 0, 2)))

    @pl.when(first)
    def _():
        late()
        build(left=True)

    for side in FORWARD:
        vector_copies[side].wait_recv()
    first_step((0,))
    second_step(((0, 1, 4), (1, 0, 1)))
    third_step(((0, 2, 4), (1, 0, 2)))

    for side in SIDES:
        feature_copies[side].wait_send()
        vector_copies[side].wait_send()


def per_device(features, pair_mask, w_update, w_atom, w_pair, slot_bias, w_block, trial):
    pair_mask = pair_mask.transpose(2, 0, 1)
    w_block = w_block.T
    rows, columns, _, width = trial.shape
    trial = trial.transpose(0, 2, 1, 3).reshape(rows, ORBITALS * columns, width)
    halves = (2, rows, ORBITALS * columns, 128)
    vectors = (10, 14, PAD, 256)
    sides = pltpu.SemaphoreType.DMA((len(SIDES),))
    filtered = pl.pallas_call(
        kernel,
        name="filter",
        out_shape=jax.ShapeDtypeStruct((rows * ORBITALS * 2 * columns, 128), F32),
        in_specs=[pl.BlockSpec(memory_space=pltpu.HBM)] * 8,
        out_specs=pl.BlockSpec(memory_space=pltpu.VMEM),
        scratch_shapes=[
            pltpu.VMEM(features.shape, BF16),
            pltpu.VMEM(pair_mask.shape, jnp.int32),
            pltpu.VMEM(w_update.shape, BF16),
            pltpu.VMEM(w_atom.shape, BF16),
            pltpu.VMEM(w_pair.shape, BF16),
            pltpu.VMEM(slot_bias.shape, F32),
            pltpu.VMEM(w_block.shape, BF16),
            pltpu.VMEM(halves, F32),
            pltpu.VMEM((9, 32, 256), BF16),
            pltpu.VMEM(vectors, BF16),
            pltpu.VMEM(vectors, BF16),
            pltpu.VMEM(vectors, BF16),
            pltpu.VMEM(vectors, BF16),
            pltpu.VMEM(vectors, F32),
            pltpu.VMEM(vectors, F32),
            pltpu.VMEM((8, 128, 256), BF16),
            pltpu.VMEM((2, 160, 192), BF16),
            pltpu.VMEM((2, 160, 192), BF16),
            pltpu.VMEM((10, 16, 128), F32),
            pltpu.VMEM((10, 16, 128), F32),
            pltpu.VMEM((10, 16, 128), F32),
            pltpu.VMEM((7, 8, 8, 256), F32),
            pltpu.VMEM((3, 2, 512, 128), F32),
            pltpu.VMEM((3, 8, 128, 256), BF16),
            pltpu.SemaphoreType.DMA((9,)),
            pltpu.SemaphoreType.REGULAR,
            sides,
            sides,
            sides,
            sides,
        ],
        compiler_params=pltpu.CompilerParams(
            collective_id=0, has_side_effects=True, vmem_limit_bytes=40 * 2**20
        ),
    )(
        *(
            pltpu.with_memory_space_constraint(array, pltpu.HBM)
            for array in (features, pair_mask, w_update, w_atom, w_pair, slot_bias, w_block, trial)
        )
    )
    filtered = filtered.reshape(rows, ORBITALS, 2, columns, 128).transpose(0, 1, 3, 2, 4)
    return filtered.reshape(rows, ORBITALS, columns, width).transpose(0, 2, 1, 3)


def solution(mesh):
    return jax.shard_map(
        per_device,
        mesh=mesh,
        in_specs=(
            P("px", "py", None),
            P("px", "py", None),
            P(),
            P(),
            P(),
            P(),
            P(),
            P("px", "py", None, None),
        ),
        out_specs=P("px", "py", None, None),
        check_vma=False,
    )
```
